32 devices in a mesh: tok: 4 (over y, x), wa: 8 (over z, core).
Axes of the slice: x: 2, y: 2, z: 4, core: 2. Of those that a mesh axis runs over, the one named last changes fastest.
Arguments:
- prompt_in: bfloat16 [8, 1024, 1024], P('wa', 'tok'), may hold values from -6 to 6
- cont_in: bfloat16 [8, 4, 256, 1024], P('wa', 'tok'), may hold values from -6 to 6
- first_gain: bfloat16 [2, 1024], P(None, 'wa'), may hold values from 0.25 to 1.75
- first_shift: bfloat16 [2, 1024], P(None, 'wa'), may hold values from -1.5 to 1.5
- qkv_weight: bfloat16 [2, 1024, 3072], P(None, 'wa'), may hold values from -0.1875 to 0.1875
- qv_bias: bfloat16 [2, 2048], P(None, 'wa'), may hold values from -1.5 to 1.5
- mix_weight: bfloat16 [2, 1024, 1024], P(None, 'wa'), may hold values from -2 to 2
- mix_bias: bfloat16 [2, 1024], P(None, 'wa'), may hold values from -1.5 to 1.5
- second_gain: bfloat16 [2, 1024], P(None, 'wa'), may hold values from 0.25 to 1.75
- second_shift: bfloat16 [2, 1024], P(None, 'wa'), may hold values from -1.5 to 1.5
- expand_weight: bfloat16 [2, 1024, 4096], P(None, 'wa'), may hold values from -0.1875 to 0.1875
- expand_bias: bfloat16 [2, 4096], P(None, 'wa'), may hold values from -1.5 to 1.5
- reduce_weight: bfloat16 [2, 4096, 1024], P(None, 'wa'), may hold values from -0.09375 to 0.09375
- reduce_bias: bfloat16 [2, 1024], P(None, 'wa'), may hold values from -1.5 to 1.5
- owners: int32 [8, 4], P('wa'), may hold values from 0 to 3, each once within a row
- prompt_cot: bfloat16 [8, 1024, 1024], P('wa', 'tok'), may hold values from -6 to 6
- cont_cot: bfloat16 [8, 4, 256, 1024], P('wa', 'tok'), may hold values from -6 to 6
Outputs:
- prompt_out: float32 [8, 1024, 1024], P('wa', 'tok')
- cont_out: float32 [8, 4, 256, 1024], P('wa', 'tok')
- prompt_grad: float32 [8, 1024, 1024], P('wa', 'tok')
- cont_grad: float32 [8, 4, 256, 1024], P('wa', 'tok')
- grad_first_gain: float32 [2, 1024], P(None, 'wa')
- grad_first_shift: float32 [2, 1024], P(None, 'wa')
- grad_qkv_weight: float32 [2, 1024, 3072], P(None, 'wa')
- grad_qv_bias: float32 [2, 2048], P(None, 'wa')
- grad_mix_weight: float32 [2, 1024, 1024], P(None, 'wa')
- grad_mix_bias: float32 [2, 1024], P(None, 'wa')
- grad_second_gain: float32 [2, 1024], P(None, 'wa')
- grad_second_shift: float32 [2, 1024], P(None, 'wa')
- grad_expand_weight: float32 [2, 1024, 4096], P(None, 'wa')
- grad_expand_bias: float32 [2, 4096], P(None, 'wa')
- grad_reduce_weight: float32 [2, 4096, 1024], P(None, 'wa')
- grad_reduce_bias: float32 [2, 1024], P(None, 'wa')
The draws below stay inside these ranges and needn't reach their ends.
Inputs may be any that keep to these rules, and one draw needn't show every extreme that they name: Row w of owners is a permutation of 0 to 3: device t along tok holds block owners[w, t] of prompt w.
All inputs are finite; a program needn't handle non-finite values.
Results may differ from the reference program's by a relative error of at most 0.015.
Values may be sent and summed in bfloat16 or wider, within the bound.
No kernel may reach another device: no remote copies, remote signals or barrier semaphores. Data moves between devices by JAX's collectives and lax.ppermute only.
A program may use at most 320 MiB of HBM per device.

```python
import jax
import jax.numpy as jnp
from jax import lax

D = 1024
HEADS = 16
HEAD = 64
FF = 4096
LAYERS = 2
PBLK = 256
CLEN = 256
PROMPT = 1024
N_TOK = 4
N_WA = 8


def raised(values, own_key, source, target, shards_of, factor):
    def block_of(dim):
        return (jnp.arange(values.shape[dim]) // (values.shape[dim] // shards_of)).reshape((-1,) + (1,) * (values.ndim - 1 - dim))

    near = jax.random.permutation(own_key, shards_of)[block_of(target)]
    other_side = (block_of(target) + shards_of // 2) % shards_of
    return jnp.where((block_of(source) == near) | (block_of(source) == other_side), factor * values, values)


def levels(key, shape, cuts, least, largest):
    def one(position, shards_of):
        heights = jax.random.uniform(jax.random.fold_in(jax.random.fold_in(key, 6), position), (shards_of,), jnp.float32, least / len(cuts), largest / len(cuts))
        return jnp.repeat(jnp.exp(heights), shape[position] // shards_of).reshape((-1,) + (1,) * (len(shape) - position - 1))

    factor_of = one(*cuts[0])
    for cut in cuts[1:]:
        factor_of = factor_of * one(*cut)
    return factor_of


def gaussian(rng, extent, width, limit, pieces=(), held_as=jnp.bfloat16):
    values = width * jax.random.normal(rng, extent, jnp.float32)
    if pieces:
        values = values * levels(rng, extent, pieces, -0.22, 0.18)
    return jnp.clip(values, -limit, limit).astype(held_as)


def gaussian_with(key, extent, deviation, limit, pieces, heavy, kind=jnp.bfloat16):
    entries = deviation * jax.random.normal(key, extent, jnp.float32)
    if pieces:
        entries = entries * levels(key, extent, pieces, -0.22, 0.18)
    return jnp.clip(raised(entries, jax.random.fold_in(key, 3), *heavy), -limit, limit).astype(kind)


def setup_inputs(seed: int = 0) -> dict:
    key_of = jax.random.split(jax.random.key(seed), 18)
    return {
        "prompt_in": gaussian(key_of[0], (N_WA, PROMPT, D), 1.0, 6.0, ((0, 8), (1, 4))),
        "cont_in": gaussian(key_of[1], (N_WA, N_TOK, CLEN, D), 1.0, 6.0, ((0, 8), (1, 4))),
        "first_gain": jnp.clip(1.0 + 0.15 * jax.random.normal(key_of[2], (LAYERS, D), jnp.float32), 0.25, 1.75).astype(jnp.bfloat16),
        "first_shift": gaussian(key_of[3], (LAYERS, D), 0.3, 1.5, ((1, 8),)),
        "qkv_weight": gaussian(key_of[4], (LAYERS, D, 3 * D), D ** -0.5, 0.1875, ((1, 8),)),
        "qv_bias": gaussian(key_of[5], (LAYERS, 2 * D), 0.3, 1.5, ((1, 8),)),
        "mix_weight": gaussian(key_of[6], (LAYERS, D, D), (max(D // 128, 2)) ** -0.5, 2.0, ((1, 8),)),
        "mix_bias": gaussian(key_of[7], (LAYERS, D), 0.3, 1.5, ((1, 8),)),
        "second_gain": jnp.clip(1.0 + 0.15 * jax.random.normal(key_of[8], (LAYERS, D), jnp.float32), 0.25, 1.75).astype(jnp.bfloat16),
        "second_shift": gaussian(key_of[9], (LAYERS, D), 0.3, 1.5, ((1, 8),)),
        "expand_weight": gaussian(key_of[10], (LAYERS, D, FF), D ** -0.5, 0.1875, ((1, 8),)),
        "expand_bias": gaussian(key_of[11], (LAYERS, FF), 0.3, 1.5, ((1, 8),)),
        "reduce_weight": gaussian(key_of[12], (LAYERS, FF, D), FF ** -0.5, 0.09375, ((1, 8),)),
        "reduce_bias": gaussian(key_of[13], (LAYERS, D), 0.3, 1.5, ((1, 8),)),
        "owners": jax.vmap(lambda own: jax.random.permutation(own, N_TOK))(jax.random.split(key_of[14], N_WA)).reshape((N_WA, N_TOK)).astype(jnp.int32),
        "prompt_cot": gaussian_with(key_of[15], (N_WA, PROMPT, D), 1.0, 6.0, ((0, 8), (1, 4)), (0, 2, 8, 2.0)),
        "cont_cot": gaussian_with(key_of[16], (N_WA, N_TOK, CLEN, D), 1.0, 6.0, ((0, 8), (1, 4)), (0, 3, 8, 2.0)),
    }


@jax.custom_vjp
def low(v):
    return lax.optimization_barrier(v.astype(jnp.bfloat16)).astype(jnp.float32)

@jax.custom_vjp
def low_back(v):
    return v

def low_keep(v):
    return (low(v), None)

def low_pass(kept, grad):
    return (grad,)

def back_keep(v):
    return (v, None)

def back_low(kept, grad):
    return (low(grad),)
low.defvjp(low_keep, low_pass)
low_back.defvjp(back_keep, back_low)
epsilon = 1e-05
negative = -1e+30

def matmul(left, right):
    return jnp.dot(left, right, precision=lax.Precision.HIGHEST, preferred_element_type=jnp.float32)

def normalize(stream, gain, shift):
    average = lax.optimization_barrier(jnp.mean(stream, -1, keepdims=True))
    centred = stream - average
    variance = lax.optimization_barrier(jnp.mean(centred * centred, -1, keepdims=True))
    return centred * lax.rsqrt(variance + epsilon) * gain + shift

def split_heads(matrix):
    return matrix.reshape(matrix.shape[0], HEADS, HEAD).transpose(1, 0, 2)

def attention(queries, key_rows, value_rows, prompt_pos):
    scaling = HEAD ** (-0.5)
    prompt_mask = prompt_pos[None, :] <= prompt_pos[:, None]
    steps_own = jnp.arange(CLEN, dtype=jnp.int32)
    own_mask = steps_own[None, :] <= steps_own[:, None]
    full_mask = jnp.concatenate([jnp.ones((CLEN, PROMPT), dtype=bool), own_mask], -1)

    def one_head(operands):
        head_queries, head_keys, head_values = operands
        prompt_queries = head_queries[:PROMPT]
        prompt_keys = head_keys[:PROMPT]
        prompt_values = head_values[:PROMPT]
        cont_queries = head_queries[PROMPT:].reshape(N_TOK, CLEN, HEAD)
        cont_keys = head_keys[PROMPT:].reshape(N_TOK, CLEN, HEAD)
        cont_values = head_values[PROMPT:].reshape(N_TOK, CLEN, HEAD)
        scores = low_back(matmul(prompt_queries, prompt_keys.T) * scaling)
        weights = jax.nn.softmax(jnp.where(prompt_mask, scores, negative), axis=-1)
        prompt_result = matmul(low(weights), prompt_values)
        far_scores = jnp.einsum('nqd,kd->nqk', cont_queries, prompt_keys, precision=lax.Precision.HIGHEST)
        near_scores = jnp.einsum('nqd,nkd->nqk', cont_queries, cont_keys, precision=lax.Precision.HIGHEST)
        joined = low_back(jnp.concatenate([far_scores, near_scores], -1) * scaling)
        cont_weights = low(jax.nn.softmax(jnp.where(full_mask[None], joined, negative), axis=-1))
        cont_result = jnp.einsum('nqk,kd->nqd', cont_weights[..., :PROMPT], prompt_values, precision=lax.Precision.HIGHEST)
        cont_result = cont_result + jnp.einsum('nqk,nkd->nqd', cont_weights[..., PROMPT:], cont_values, precision=lax.Precision.HIGHEST)
        return jnp.concatenate([prompt_result, cont_result.reshape(N_TOK * CLEN, HEAD)], 0)
    results = lax.map(jax.checkpoint(one_head), (split_heads(queries), split_heads(key_rows), split_heads(value_rows)))
    return results.transpose(1, 0, 2).reshape(queries.shape[0], D)

def layer(params, stream, prompt_pos):
    first_gain, first_shift, qkv_weight, qv_bias, mix_weight, mix_bias, second_gain, second_shift, expand_weight, expand_bias, reduce_weight, reduce_bias = params
    normed = low(normalize(stream, first_gain, first_shift))
    mixed = matmul(normed, qkv_weight)
    queries = low_back(low(mixed[:, :D] + qv_bias[:D]))
    key_rows = low_back(low(mixed[:, D:2 * D]))
    value_rows = low_back(low(mixed[:, 2 * D:] + qv_bias[D:]))
    attended = low_back(low(attention(queries, key_rows, value_rows, prompt_pos)))
    middle = stream + low_back(matmul(attended, mix_weight) + mix_bias)
    second = low(normalize(middle, second_gain, second_shift))
    hidden = low_back(matmul(second, expand_weight) + expand_bias)
    active = low(jax.nn.gelu(hidden, approximate=True))
    return middle + low_back(matmul(active, reduce_weight) + reduce_bias)

def forward(params, prompt_rows, cont_rows, prompt_pos):
    stream = jnp.concatenate([prompt_rows, cont_rows.reshape(N_TOK * CLEN, D)], 0)
    for layer_index in range(LAYERS):
        stream = layer(tuple((piece[layer_index] for piece in params)), stream, prompt_pos)
    return (stream[:PROMPT], stream[PROMPT:].reshape(N_TOK, CLEN, D))

def reference(prompt_in, cont_in, first_gain, first_shift, qkv_weight, qv_bias, mix_weight, mix_bias, second_gain, second_shift, expand_weight, expand_bias, reduce_weight, reduce_bias, owners, prompt_cot, cont_cot):
    params = tuple((piece.astype(jnp.float32) for piece in (first_gain, first_shift, qkv_weight, qv_bias, mix_weight, mix_bias, second_gain, second_shift, expand_weight, expand_bias, reduce_weight, reduce_bias)))

    def group(totals, inputs):
        prompt_rows, cont_rows, block_order, prompt_seed, cont_seed = inputs
        offsets = jnp.arange(PBLK, dtype=jnp.int32)
        prompt_pos = (block_order.astype(jnp.int32)[:, None] * PBLK + offsets[None, :]).reshape(PROMPT)

        def run(weights_in, first_rows, later_rows):
            return forward(weights_in, first_rows, later_rows, prompt_pos)
        outputs, pullback = jax.vjp(run, params, prompt_rows.astype(jnp.float32), cont_rows.astype(jnp.float32))
        grads = pullback((prompt_seed.astype(jnp.float32), cont_seed.astype(jnp.float32)))
        totals = jax.tree.map(jnp.add, totals, grads[0])
        return (totals, (outputs[0], outputs[1], grads[1], grads[2]))
    start = tuple((jnp.zeros_like(piece) for piece in params))
    totals, (prompt_out, cont_out, prompt_grad, cont_grad) = lax.scan(group, start, (prompt_in, cont_in, owners, prompt_cot, cont_cot))
    return (prompt_out, cont_out, prompt_grad, cont_grad, totals[0], totals[1], totals[2], totals[3], totals[4], totals[5], totals[6], totals[7], totals[8], totals[9], totals[10], totals[11])
```

```python
import functools

import jax
import jax.numpy as jnp
from jax import lax
from jax.experimental import pallas as pl
from jax.experimental.pallas import tpu as pltpu
from jax.sharding import PartitionSpec as P

HEAD = 64
PAIR = 2 * HEAD
LAYERS = 2
EPSILON = 1e-05
NEGATIVE = -1e30
CURVE = 0.7978845608028654
CUBIC = 0.044715
F32 = jnp.float32
BF16 = jnp.bfloat16

V_FG, V_FS, V_QKV, V_MB, V_SG, V_SS, V_RB, V_EB = 0, 1, 2, 5, 6, 7, 8, 9


def dot(left, right):
    return jnp.dot(left, right, preferred_element_type=F32)


def dot_nt(left, right):
    return lax.dot_general(left, right, (((1,), (1,)), ((), ())), preferred_element_type=F32)


def dot_tn(left, right):
    return lax.dot_general(left, right, (((0,), (0,)), ((), ())), preferred_element_type=F32)


def params(semantics=("arbitrary",), mib=56):
    return pltpu.CompilerParams(dimension_semantics=semantics, vmem_limit_bytes=mib * 2**20)


def cost(flops, nbytes, trans=0):
    return pl.CostEstimate(flops=int(flops), bytes_accessed=int(nbytes), transcendentals=int(trans))


def center(rows):
    centred = rows - jnp.mean(rows, -1, keepdims=True)
    inverse = lax.rsqrt(jnp.mean(centred * centred, -1, keepdims=True) + EPSILON)
    return centred * inverse, inverse


def norm_pull(rows, gain, grad):
    normal, inverse = center(rows)
    inner = grad * gain
    term = inverse * (
        inner
        - jnp.mean(inner, -1, keepdims=True)
        - normal * jnp.mean(inner * normal, -1, keepdims=True)
    )
    return term, jnp.sum(grad * normal, 0, keepdims=True), jnp.sum(grad, 0, keepdims=True)


def whole(shape):
    return pl.BlockSpec(shape, lambda *_: (0,) * len(shape))


def vector(width, place):
    return pl.BlockSpec((1, width), lambda *_: (0, place))


def qkv_kernel(x_ref, gain_ref, shift_ref, bias_ref, w_ref, out_ref, normed_ref):
    @pl.when(pl.program_id(0) == 0)
    def _():
        normal, _ = center(x_ref[...])
        normed_ref[...] = (normal * gain_ref[...] + shift_ref[...]).astype(BF16)

    out_ref[...] = (dot(normed_ref[...], w_ref[...]) + bias_ref[...]).astype(BF16)


def qkv_forward(stream, vec, weights, place):
    rows, width = stream.shape
    block = 512
    steps = 3 * width // block
    return pl.pallas_call(
        qkv_kernel,
        grid=(steps,),
        in_specs=[
            whole((rows, width)),
            vector(width, V_FG),
            vector(width, V_FS),
            pl.BlockSpec((1, block), lambda j: (0, V_QKV * width // block + j)),
            pl.BlockSpec((width, block), lambda j: (0, place // block + j)),
        ],
        out_specs=[pl.BlockSpec((rows, block), lambda j: (0, j)), whole((rows, width))],
        out_shape=[
            jax.ShapeDtypeStruct((rows, 3 * width), BF16),
            jax.ShapeDtypeStruct((rows, width), BF16),
        ],
        compiler_params=params(),
        cost_estimate=cost(6 * rows * width * width, 16 * 2**20),
        name="qkv_forward",
    )(stream, vec, vec, vec, weights)


def offsets(rows):
    return lax.broadcasted_iota(jnp.int32, (rows, rows), 0) - lax.broadcasted_iota(
        jnp.int32, (rows, rows), 1
    )


def head_lanes(block, half):
    lanes = lax.broadcasted_iota(jnp.int32, block.shape, 1) // HEAD
    return jnp.where(lanes == half, block, jnp.zeros_like(block))


def attend_kernel(pb, far, *refs):
    thr_ref, q_ref, k_ref, v_ref = refs[:4]
    far_refs = refs[4 : 4 + far]
    out_ref, lse_ref = refs[4 + far :]
    steps = offsets(pb)
    keys = [k_ref[:pb, :]] + [ref[0] for ref in far_refs]
    values = [v_ref[:pb, :]] + [ref[1] for ref in far_refs]
    total = None
    for half in range(2):
        q = head_lanes(q_ref[...], half) * jnp.asarray(HEAD**-0.5, BF16)
        lefts, rights = [], []
        for j, k in enumerate(keys):
            s = dot_nt(k, q)
            lefts.append(jnp.where(steps <= thr_ref[j], s[:, :pb], NEGATIVE))
            rights.append(s[:, pb:])
        own = jnp.where(steps <= 0, dot_nt(k_ref[pb:, :], q[pb:, :]), NEGATIVE)
        top_p = jnp.max(functools.reduce(jnp.maximum, lefts), 0, keepdims=True)
        top_c = jnp.max(functools.reduce(jnp.maximum, rights + [own]), 0, keepdims=True)
        sum_p = jnp.zeros((1, pb), F32)
        own = jnp.exp(own - top_c)
        sum_c = jnp.sum(own, 0, keepdims=True)
        acc_p = jnp.zeros((PAIR, pb), F32)
        acc_c = dot_tn(head_lanes(v_ref[pb:, :], half), own.astype(BF16))
        for j, v in enumerate(values):
            v = head_lanes(v, half)
            left = jnp.exp(lefts[j] - top_p)
            right = jnp.exp(rights[j] - top_c)
            sum_p += jnp.sum(left, 0, keepdims=True)
            sum_c += jnp.sum(right, 0, keepdims=True)
            acc_p += dot_tn(v, left.astype(BF16))
            acc_c += dot_tn(v, right.astype(BF16))
        lse_ref[half, :, :] = jnp.concatenate(
            [top_p + jnp.log(sum_p), top_c + jnp.log(sum_c)], 1
        )
        part = jnp.concatenate([acc_p / sum_p, acc_c / sum_c], 1)
        total = part if total is None else total + part
    out_ref[...] = total.T.astype(BF16)


def attend_forward(thr, qkv, far, part, parts):
    rows, width = qkv.shape[0], qkv.shape[1] // 3
    pb = rows // 2
    pairs = width // PAIR // parts
    place = lambda kind: pl.BlockSpec((rows, PAIR), lambda i: (0, (kind * parts + part) * pairs + i))
    block = pl.BlockSpec((2, pb, PAIR), lambda i: (0, 0, i))
    return pl.pallas_call(
        functools.partial(attend_kernel, pb, len(far)),
        grid=(pairs,),
        in_specs=[pl.BlockSpec(memory_space=pltpu.SMEM), place(0), place(1), place(2)]
        + [block] * len(far),
        out_specs=[
            pl.BlockSpec((rows, PAIR), lambda i: (0, i)),
            pl.BlockSpec((2, 1, rows), lambda i: (i, 0, 0)),
        ],
        out_shape=[
            jax.ShapeDtypeStruct((rows, width // parts), BF16),
            jax.ShapeDtypeStruct((2 * pairs, 1, rows), F32),
        ],
        compiler_params=params(),
        cost_estimate=cost(
            48 * rows * (len(far) + 2) * pb * width // parts,
            10 * 2**20 // parts,
            rows * (len(far) + 1) * pb * 16 // parts,
        ),
        name="attend_forward",
    )(thr, qkv, qkv, qkv, *far)


def attend_pull_kernel(pb, far, *refs):
    thr_ref, q_ref, k_ref, v_ref = refs[:4]
    far_refs = refs[4 : 4 + far]
    lse_ref, do_ref, o_ref = refs[4 + far : 7 + far]
    dq_ref, dcont_ref = refs[7 + far : 9 + far]
    dfar_refs = refs[9 + far :]
    steps = offsets(pb)
    scale = HEAD**-0.5
    keys = [k_ref[:pb, :]] + [ref[0] for ref in far_refs]
    values = [v_ref[:pb, :]] + [ref[1] for ref in far_refs]
    both = (do_ref[...].astype(F32) * o_ref[...].astype(F32)).T
    dq = jnp.zeros((PAIR, 2 * pb), F32)
    dks = [jnp.zeros((pb, PAIR), F32) for _ in keys]
    dvs = [jnp.zeros((pb, PAIR), F32) for _ in keys]
    dkc = jnp.zeros((pb, PAIR), F32)
    dvc = jnp.zeros((pb, PAIR), F32)
    dqc = jnp.zeros((PAIR, pb), F32)
    for half in range(2):
        q = head_lanes(q_ref[...], half) * jnp.asarray(scale, BF16)
        do = head_lanes(do_ref[...], half)
        lse = lse_ref[half, :, :]
        delta = jnp.sum(both[half * HEAD : (half + 1) * HEAD, :], 0, keepdims=True)
        for j, (k, v) in enumerate(zip(keys, values)):
            s = dot_nt(k, q)
            left = jnp.where(steps <= thr_ref[j], s[:, :pb], NEGATIVE)
            p = jnp.exp(jnp.concatenate([left, s[:, pb:]], 1) - lse)
            dp = dot_nt(v, do)
            ds = (p * (dp - delta)).astype(BF16)
            dvs[j] += dot(p.astype(BF16), do)
            dks[j] += dot(ds, q)
            dq += dot_tn(head_lanes(k, half), ds)
        kc, vc = k_ref[pb:, :], v_ref[pb:, :]
        s = jnp.where(steps <= 0, dot_nt(kc, q[pb:, :]), NEGATIVE)
        p = jnp.exp(s - lse[:, pb:])
        dp = dot_nt(vc, do[pb:, :])
        ds = (p * (dp - delta[:, pb:])).astype(BF16)
        dvc += dot(p.astype(BF16), do[pb:, :])
        dkc += dot(ds, q[pb:, :])
        dqc += dot_tn(head_lanes(kc, half), ds)
    for ref, dk, dv in zip(dfar_refs, dks, dvs):
        ref[0] = dk.astype(BF16)
        ref[1] = dv.astype(BF16)
    dcont_ref[0] = dkc.astype(BF16)
    dcont_ref[1] = dvc.astype(BF16)
    dq = jnp.concatenate([dq[:, :pb], dq[:, pb:] + dqc], 1)
    dq_ref[...] = (dq.T * scale).astype(BF16)


def attend_backward(thr, qkv, far, lse, do, attended, part, parts):
    rows, width = qkv.shape[0], qkv.shape[1] // 3
    pb = rows // 2
    pairs = width // PAIR // parts
    place = lambda kind: pl.BlockSpec((rows, PAIR), lambda i: (0, (kind * parts + part) * pairs + i))
    block = pl.BlockSpec((2, pb, PAIR), lambda i: (0, 0, i))
    column = pl.BlockSpec((rows, PAIR), lambda i: (0, i))
    pieces = len(far) + 2
    return pl.pallas_call(
        functools.partial(attend_pull_kernel, pb, len(far)),
        grid=(pairs,),
        in_specs=[pl.BlockSpec(memory_space=pltpu.SMEM), place(0), place(1), place(2)]
        + [block] * len(far)
        + [pl.BlockSpec((2, 1, rows), lambda i: (i, 0, 0)), place(0), column],
        out_specs=[column] + [block] * pieces,
        out_shape=[jax.ShapeDtypeStruct((rows, width // parts), BF16)]
        + [jax.ShapeDtypeStruct((2, pb, width // parts), BF16)] * pieces,
        compiler_params=params(),
        cost_estimate=cost(
            80 * rows * pieces * pb * width // parts,
            18 * 2**20 // parts,
            rows * pieces * pb * 16 // parts,
        ),
        name="attend_backward",
    )(thr, qkv, qkv, qkv, *far, lse, do, attended)


def gather_slabs(target, source):
    span, width = source.shape[0], target.shape[1]
    for a in range(target.shape[0] // span):
        target[a * span : (a + 1) * span, :] = source[:, a * width : (a + 1) * width]


def feed_kernel(
    parts, x_ref, *refs
):
    att_refs = refs[:parts]
    (wm_ref, mb_ref, gain_ref, shift_ref, eb_ref, rb_ref, we_ref, wr_ref,
     out_ref, middle_ref, second_ref, hidden_ref, wr_scr) = refs[parts:]

    @pl.when(pl.program_id(0) == 0)
    def _():
        middle = x_ref[...] + mb_ref[...]
        size = att_refs[0].shape[1]
        for part, ref in enumerate(att_refs):
            middle += dot(ref[...], wm_ref[part * size : (part + 1) * size, :])
        middle_ref[...] = middle
        normal, _ = center(middle)
        second_ref[...] = (normal * gain_ref[...] + shift_ref[...]).astype(BF16)
        out_ref[...] = middle + rb_ref[...]

    gather_slabs(wr_scr, wr_ref)
    hidden = dot(second_ref[...], we_ref[...]) + eb_ref[...]
    hidden_ref[...] = hidden.astype(BF16)
    active = 0.5 * hidden * (1.0 + jnp.tanh(CURVE * (hidden + CUBIC * hidden * hidden * hidden)))
    out_ref[...] += dot(active.astype(BF16), wr_scr[...])


def feed_forward(steps, stream, attended, vec, weights):
    rows, width = stream.shape
    ff = 4 * width
    block = ff // steps
    span = width // steps
    (wr, reduce_at), (we, expand_at), (wm, mix_at) = weights
    return pl.pallas_call(
        functools.partial(feed_kernel, len(attended)),
        grid=(steps,),
        in_specs=[whole((rows, width))]
        + [whole(piece.shape) for piece in attended]
        + [
            pl.BlockSpec((width, width), lambda j: (0, mix_at // width)),
            vector(width, V_MB),
            vector(width, V_SG),
            vector(width, V_SS),
            pl.BlockSpec((1, block), lambda j: (0, V_EB * width // block + j)),
            vector(width, V_RB),
            pl.BlockSpec((width, block), lambda j: (0, expand_at // block + j)),
            pl.BlockSpec((span, ff), lambda j: (j, reduce_at // ff)),
        ],
        out_specs=[
            whole((rows, width)),
            whole((rows, width)),
            whole((rows, width)),
            pl.BlockSpec((rows, block), lambda j: (0, j)),
        ],
        out_shape=[
            jax.ShapeDtypeStruct((rows, width), F32),
            jax.ShapeDtypeStruct((rows, width), F32),
            jax.ShapeDtypeStruct((rows, width), BF16),
            jax.ShapeDtypeStruct((rows, ff), BF16),
        ],
        scratch_shapes=[pltpu.VMEM((block, width), BF16)],
        compiler_params=params(),
        cost_estimate=cost(18 * rows * width * width, 30 * 2**20, rows * ff),
        name="feed_forward",
    )(stream, *attended, wm, vec, vec, vec, vec, vec, we, wr)


def put_rows(refs, grad, core):
    if len(refs) == 1:
        refs[0][...] = grad
        return
    mine, other = refs
    planes, span, block = mine.shape
    split = grad.reshape(planes, 2, span, block)
    first = core == 0
    mine[...] = jnp.where(first, split[:, 0], split[:, 1])
    other[...] = jnp.where(first, split[:, 1], split[:, 0])


def grad_outs(steps, width, columns, block, index, apart):
    if not apart:
        return [pl.BlockSpec((width, block), lambda j: (0, index(j)))], [
            jax.ShapeDtypeStruct((width, columns), BF16)
        ]
    shape = (steps // 2, width // steps)
    spec = pl.BlockSpec(shape + (block,), lambda j: (0, 0, index(j)))
    return [spec] * 2, [jax.ShapeDtypeStruct(shape + (columns,), BF16)] * 2


def feed_pull_kernel(steps, parts, outs, core_ref, gs_ref, *refs):
    att_refs = refs[:parts]
    hidden_ref, second_ref, middle_ref, gain_ref, we_ref, wr_ref, wm_ref = refs[parts : parts + 7]
    refs = refs[parts + 7 :]
    dwe_refs, dwr_refs = refs[:outs], refs[outs : 2 * outs]
    (gm_ref, gatt_ref, deb_ref, drb_ref, dsg_ref, dss_ref, dmb_ref,
     gb_scr, sec_scr, wr_scr, acc_scr, att_scr) = refs[2 * outs :]
    step = pl.program_id(0)
    core = core_ref[0]
    width = gs_ref.shape[1]
    block = wr_scr.shape[0]

    @pl.when(step == 0)
    def _():
        branch = gs_ref[...].astype(BF16)
        gb_scr[...] = branch
        drb_ref[...] = jnp.sum(branch.astype(F32), 0, keepdims=True)
        sec_scr[...] = second_ref[...].T
        acc_scr[...] = jnp.zeros_like(acc_scr)
        size = att_refs[0].shape[1]
        for part, ref in enumerate(att_refs):
            att_scr[part * size : (part + 1) * size, :] = ref[...].T

    @pl.when(step < steps)
    def _():
        gather_slabs(wr_scr, wr_ref)
        branch = gb_scr[...]
        grad_active = dot_nt(branch, wr_scr[...])
        v = hidden_ref[...].astype(F32)
        square = v * v
        t = jnp.tanh(CURVE * v * (1.0 + CUBIC * square))
        half = 0.5 + 0.5 * t
        slope = half + 0.5 * v * (1.0 - t * t) * (CURVE * (1.0 + 3 * CUBIC * square))
        grad_hidden = (grad_active * slope).astype(BF16)
        active = (v * half).astype(BF16)
        deb_ref[...] = jnp.sum(grad_hidden.astype(F32), 0, keepdims=True)
        wr_scr[...] = dot_tn(active, branch).astype(BF16)
        span = block * width // (4 * width)

        def put_slabs(target):
            for a in range(4):
                target(slice(a * width, (a + 1) * width), wr_scr[a * span : (a + 1) * span, :])

        if outs == 1:
            def one(columns, value):
                dwr_refs[0][:, columns] = value

            put_slabs(one)
        else:
            for place, ref in enumerate(dwr_refs):
                @pl.when(step % 2 == (core if place == 0 else 1 - core))
                def _(ref=ref):
                    def one(columns, value):
                        ref[0, :, columns] = value

                    put_slabs(one)

        put_rows(dwe_refs, dot(sec_scr[...], grad_hidden).astype(BF16), core)
        acc_scr[...] += dot_nt(grad_hidden, we_ref[...])

    @pl.when(step == steps)
    def _():
        term, dgain, dshift = norm_pull(middle_ref[...], gain_ref[...], acc_scr[...])
        dsg_ref[...] = dgain
        dss_ref[...] = dshift
        grad_middle = gs_ref[...] + term
        gm_ref[...] = grad_middle
        grad_mix = grad_middle.astype(BF16)
        gb_scr[...] = grad_mix
        dmb_ref[...] = jnp.sum(grad_mix.astype(F32), 0, keepdims=True)
        gatt_ref[...] = dot_nt(grad_mix, wm_ref[...]).astype(BF16)

    @pl.when(step >= steps)
    def _():
        start = pl.multiple_of((step - steps) * block, block)
        put_rows(dwe_refs, dot(att_scr[...], gb_scr[:, pl.ds(start, block)]).astype(BF16), core)


def feed_backward(steps, core, grad_stream, hidden, second, middle, attended, vec, weights, apart):
    rows, width = grad_stream.shape
    ff = 4 * width
    block = ff // steps
    span = width // steps
    (wr, reduce_at), (we, expand_at), (wm, mix_at) = weights
    row = whole((1, width))
    small = jax.ShapeDtypeStruct((1, width), F32)
    last = lambda j: jnp.minimum(j, steps - 1)
    dwe_specs, dwe_shapes = grad_outs(steps, width, ff + width, block, lambda j: j, apart)
    if apart:
        dwr_specs = [pl.BlockSpec((1, span, ff), lambda j: (last(j) // 2, 0, 0))] * 2
        dwr_shapes = [jax.ShapeDtypeStruct((steps // 2, span, ff), BF16)] * 2
    else:
        dwr_specs = [pl.BlockSpec((span, ff), lambda j: (last(j), 0))]
        dwr_shapes = [jax.ShapeDtypeStruct((width, ff), BF16)]
    outs = len(dwe_specs)
    return pl.pallas_call(
        functools.partial(feed_pull_kernel, steps, len(attended), outs),
        grid=(steps + width // block,),
        in_specs=[pl.BlockSpec(memory_space=pltpu.SMEM), whole((rows, width))]
        + [whole(piece.shape) for piece in attended]
        + [
            pl.BlockSpec((rows, block), lambda j: (0, last(j))),
            whole((rows, width)),
            whole((rows, width)),
            vector(width, V_SG),
            pl.BlockSpec((width, block), lambda j: (0, expand_at // block + last(j))),
            pl.BlockSpec((span, ff), lambda j: (last(j), reduce_at // ff)),
            pl.BlockSpec((width, width), lambda j: (0, mix_at // width)),
        ],
        out_specs=dwe_specs
        + dwr_specs
        + [
            whole((rows, width)),
            whole((rows, width)),
            pl.BlockSpec((1, block), lambda j: (0, last(j))),
            row,
            row,
            row,
            row,
        ],
        out_shape=dwe_shapes
        + dwr_shapes
        + [
            jax.ShapeDtypeStruct((rows, width), F32),
            jax.ShapeDtypeStruct((rows, width), BF16),
            jax.ShapeDtypeStruct((1, ff), F32),
            small,
            small,
            small,
            small,
        ],
        scratch_shapes=[
            pltpu.VMEM((rows, width), BF16),
            pltpu.VMEM((width, rows), BF16),
            pltpu.VMEM((block, width), BF16),
            pltpu.VMEM((rows, width), F32),
            pltpu.VMEM((width, rows), BF16),
        ],
        compiler_params=params(),
        cost_estimate=cost(36 * rows * width * width, 50 * 2**20, rows * ff),
        name="feed_backward",
    )(core, grad_stream, *attended, hidden, second, middle, vec, we, wr, wm)


def qkv_pull_kernel(parts, sums, outs, core_ref, *refs):
    dq_refs, refs = refs[:parts], refs[parts:]
    cont_refs, refs = refs[:parts], refs[parts:]
    sum_refs, refs = refs[: parts * sums], refs[parts * sums :]
    normed_ref, x_ref, gm_ref, gain_ref, w_ref = refs[:5]
    dw_refs = refs[5 : 5 + outs]
    out_ref, dbias_ref, dgain_ref, dshift_ref, norm_scr, acc_scr, g_scr = refs[5 + outs :]
    step = pl.program_id(0)

    @pl.when(step == 0)
    def _():
        norm_scr[...] = normed_ref[...].T
        acc_scr[...] = jnp.zeros_like(acc_scr)
        for part in range(parts):
            g_scr[part] = dq_refs[part][...]
            total = sum(ref[...].astype(F32) for ref in sum_refs[part * sums : (part + 1) * sums])
            for kind in range(2):
                both = jnp.concatenate([total[kind].astype(BF16), cont_refs[part][kind]], 0)
                g_scr[(1 + kind) * parts + part] = both

    grad = g_scr[step]
    dbias_ref[...] = jnp.sum(grad.astype(F32), 0, keepdims=True)
    put_rows(dw_refs, dot(norm_scr[...], grad).astype(BF16), core_ref[0])
    acc_scr[...] += dot_nt(grad, w_ref[...])

    @pl.when(step == pl.num_programs(0) - 1)
    def _():
        term, dgain, dshift = norm_pull(x_ref[...], gain_ref[...], acc_scr[...])
        dgain_ref[...] = dgain
        dshift_ref[...] = dshift
        out_ref[...] = gm_ref[...] + term


def qkv_backward(steps, core, dqs, conts, sums, normed, stream, grad_middle, vec, weights, apart):
    rows, width = stream.shape
    parts = len(dqs)
    block = width // parts
    wq, place = weights
    small = jax.ShapeDtypeStruct((1, width), F32)
    flat = [piece for part in sums for piece in part]
    dw_specs, dw_shapes = grad_outs(steps, width, 3 * width, block, lambda j: j, apart)
    return pl.pallas_call(
        functools.partial(qkv_pull_kernel, parts, len(sums[0]), len(dw_specs)),
        grid=(3 * parts,),
        in_specs=[pl.BlockSpec(memory_space=pltpu.SMEM)]
        + [whole(piece.shape) for piece in dqs + conts + flat]
        + [
            whole((rows, width)),
            whole((rows, width)),
            whole((rows, width)),
            vector(width, V_FG),
            pl.BlockSpec((width, block), lambda j: (0, place // block + j)),
        ],
        out_specs=dw_specs
        + [
            whole((rows, width)),
            pl.BlockSpec((1, block), lambda j: (0, j)),
            whole((1, width)),
            whole((1, width)),
        ],
        out_shape=dw_shapes
        + [
            jax.ShapeDtypeStruct((rows, width), F32),
            jax.ShapeDtypeStruct((1, 3 * width), F32),
            small,
            small,
        ],
        scratch_shapes=[
            pltpu.VMEM((width, rows), BF16),
            pltpu.VMEM((rows, width), F32),
            pltpu.VMEM((3 * parts, rows, block), BF16),
        ],
        compiler_params=params(),
        cost_estimate=cost(12 * rows * width * width, 24 * 2**20),
        name="qkv_backward",
    )(core, *dqs, *conts, *flat, normed, stream, grad_middle, vec, wq)


def trade(block, axis, bits):
    return lax.ppermute(block, axis, [(i, i ^ bits) for i in range(lax.axis_size(axis))])


def pick(block, place, axis):
    return lax.dynamic_index_in_dim(block, place, axis, keepdims=False)


def added(*blocks):
    return sum(block.astype(F32) for block in blocks).astype(BF16)


def reduce_blocks(mine, other):
    planes, span, columns = mine.shape
    n_tok = lax.axis_size("tok")
    me, plane = lax.axis_index("tok"), lax.axis_index("wa") // 2
    bits = n_tok.bit_length() - 1
    got = trade(other, "wa", 1)
    cut = columns // 2
    finished = []
    for side in range(2):
        order = list(range(bits)) if side == 0 else list(reversed(range(bits)))
        shape = (planes,) + (2,) * bits + (span // n_tok, cut)
        pieces = [block[:, :, side * cut : (side + 1) * cut].reshape(shape) for block in (mine, got)]
        left = list(reversed(range(bits)))
        for bit in order:
            axis = 1 + left.index(bit)
            left.remove(bit)
            place = (me >> bit) & 1
            send = added(*[pick(piece, 1 - place, axis) for piece in pieces])
            kept = [pick(piece, place, axis) for piece in pieces]
            pieces = kept + [trade(send, "tok", 1 << bit)]
        finished.append(added(*pieces))
    block = jnp.concatenate(finished, -1)
    return added(
        pick(block, plane, 0),
        *[trade(pick(block, plane ^ step, 0), "wa", 2 * step) for step in range(1, planes)]
    )


def my_rows(shard, parts, me):
    rows = shard.shape[0] // parts
    return lax.dynamic_slice_in_dim(shard, me * rows, rows, 0)


def my_slabs(shard, parts, me):
    width = shard.shape[1]
    stacked = shard.reshape(4, shard.shape[0] // 4, width)
    rows = stacked.shape[1] // parts
    mine = lax.dynamic_slice_in_dim(stacked, me * rows, rows, 1)
    return mine.transpose(1, 0, 2).reshape(rows, 4 * width)


def local(
    prompt_in, cont_in, first_gain, first_shift, qkv_weight, qv_bias, mix_weight, mix_bias,
    second_gain, second_shift, expand_weight, expand_bias, reduce_weight, reduce_bias, owners,
    prompt_cot, cont_cot,
):
    n_tok, n_wa = lax.axis_size("tok"), lax.axis_size("wa")
    me = lax.axis_index("tok")
    core = (lax.axis_index("wa") % 2).reshape(1)
    rows = prompt_in.shape[1]
    width = prompt_in.shape[2]
    span = width // n_wa
    parts = 2
    steps = list(range(1, n_tok))
    order = owners[0]
    by_step = jnp.stack([pick(order, me ^ step, 0) for step in [0] + steps])
    thr = (by_step[0] - by_step) * rows

    small = jnp.concatenate(
        [first_gain, first_shift, qv_bias, mix_bias, second_gain, second_shift, reduce_bias, expand_bias], 1
    )
    small = lax.all_gather(small, "wa", axis=0, tiled=False)

    def spread(layer):
        def piece(start, count):
            return small[:, layer, start * span : (start + count) * span].reshape(1, -1)

        pair = piece(2, 2)
        pieces = [
            piece(0, 1), piece(1, 1), pair[:, :width], jnp.zeros((1, width), BF16), pair[:, width:],
            piece(4, 1), piece(5, 1), piece(6, 1), piece(7, 1), piece(8, 4),
        ]
        return jnp.concatenate(pieces, 1).astype(F32)

    vecs = [spread(layer) for layer in range(LAYERS)]
    both = ("wa", "tok")

    def gather(blocks):
        return lax.all_gather(jnp.concatenate(blocks, 1), both, axis=0, tiled=True)

    def piece_of(weight, layer):
        return my_rows(weight[layer], n_tok, me)

    def late(layer):
        return [my_slabs(reduce_weight[layer], n_tok, me), piece_of(expand_weight, layer)]

    first = gather([piece_of(qkv_weight, 0)])
    rest = gather(late(0) + [piece_of(mix_weight, 0)])
    after = gather(late(1) + [piece_of(qkv_weight, 1), piece_of(mix_weight, 1)])
    weights = [
        ((first, 0), ((rest, 0), (rest, 4 * width), (rest, 8 * width))),
        ((after, 8 * width), ((after, 0), (after, 4 * width), (after, 11 * width))),
    ]

    stream = jnp.concatenate([prompt_in[0], cont_in[0, 0]], 0).astype(F32)
    kept = []
    size = width // parts
    for layer in range(LAYERS):
        wq, wf = weights[layer]
        qkv, normed = qkv_forward(stream, vecs[layer], *wq)
        fars, attended, lses = [], [], []
        for part in range(parts):
            block = jnp.stack(
                [
                    qkv[:rows, kind * width + part * size : kind * width + (part + 1) * size]
                    for kind in (1, 2)
                ]
            )
            fars.append([trade(block, "tok", step) for step in steps])
        for part in range(parts):
            one, lse = attend_forward(thr, qkv, fars[part], part, parts)
            attended.append(one)
            lses.append(lse)
        result, middle, second, hidden = feed_forward(n_wa, stream, attended, vecs[layer], wf)
        kept.append((stream, normed, qkv, fars, lses, attended, middle, second, hidden))
        stream = result

    grad_stream = jnp.concatenate([prompt_cot[0], cont_cot[0, 0]], 0).astype(F32)
    totals = [None] * LAYERS
    smalls = [None] * LAYERS
    for layer in reversed(range(LAYERS)):
        wq, wf = weights[layer]
        before, normed, qkv, fars, lses, attended, middle, second, hidden = kept[layer]
        apart = layer == 0
        grads = feed_backward(
            n_wa, core, grad_stream, hidden, second, middle, attended, vecs[layer], wf, apart
        )
        outs = 2 if apart else 1
        dwe, dwr = grads[:outs], grads[outs : 2 * outs]
        grad_middle, grad_att, deb, drb, dsg, dss, dmb = grads[2 * outs :]
        dqs, conts, sums = [], [], []
        for part in range(parts):
            dq, cont, own, *far = attend_backward(
                thr, qkv, fars[part], lses[part], grad_att, attended[part], part, parts
            )
            dqs.append(dq)
            conts.append(cont)
            sums.append([own] + [trade(block, "tok", step) for step, block in zip(steps, far)])
        dwq_mine, dwq_other, grad_stream, dqb, dfg, dfs = qkv_backward(
            n_wa, core, dqs, conts, sums, normed, before, grad_middle, vecs[layer], wq, True
        )
        if apart:
            done = [reduce_blocks(*dwr), reduce_blocks(*dwe)]
        else:
            done = [
                lax.psum_scatter(block[0], "wa", scatter_dimension=0, tiled=True) for block in (dwr, dwe)
            ]
        totals[layer] = done + [reduce_blocks(dwq_mine, dwq_other)]
        dqb = jnp.concatenate([dqb[:, :width], dqb[:, 2 * width :]], 1)
        smalls[layer] = [
            piece.reshape(n_wa, -1) for piece in (dfg, dfs, dqb, dmb, dsg, dss, deb, drb)
        ]

    small = jnp.stack([jnp.concatenate(pieces, 1) for pieces in smalls], 1)
    small = lax.psum(small, both)
    small = lax.dynamic_index_in_dim(small, lax.axis_index("wa"), 0, keepdims=False)

    def vec_out(start, count):
        return small[:, start * span : (start + count) * span]

    def complete(block):
        return lax.all_gather(block, "tok", axis=0, tiled=True)

    upper = lax.psum(jnp.concatenate(totals[1][:2], 1), "tok")
    lower = complete(jnp.concatenate(totals[0][:2] + totals[1][2:], 1))
    lower_qkv = complete(totals[0][2])
    wide = 9 * width
    pairs = [(lower[:, :wide], lower_qkv), (upper, lower[:, wide:])]

    def weight_out(source, start, count):
        return jnp.stack(
            [pair[source][:, start * width : (start + count) * width] for pair in pairs], 0
        ).astype(F32)

    reduce_out = weight_out(0, 0, 4).reshape(LAYERS, span, 4, width).transpose(0, 2, 1, 3)
    return (
        stream[:rows][None],
        stream[rows:][None, None],
        grad_stream[:rows][None],
        grad_stream[rows:][None, None],
        vec_out(0, 1),
        vec_out(1, 1),
        weight_out(1, 0, 3),
        vec_out(2, 2),
        weight_out(0, 8, 1),
        vec_out(4, 1),
        vec_out(5, 1),
        vec_out(6, 1),
        weight_out(0, 4, 4),
        vec_out(7, 4),
        reduce_out.reshape(LAYERS, 4 * span, width),
        vec_out(11, 1),
    )


def solution(mesh):
    in_specs = (
        P("wa", "tok", None),
        P("wa", "tok", None, None),
        P(None, "wa"),
        P(None, "wa"),
        P(None, "wa", None),
        P(None, "wa"),
        P(None, "wa", None),
        P(None, "wa"),
        P(None, "wa"),
        P(None, "wa"),
        P(None, "wa", None),
        P(None, "wa"),
        P(None, "wa", None),
        P(None, "wa"),
        P("wa", None),
        P("wa", "tok", None),
        P("wa", "tok", None, None),
    )
    out_specs = (
        P("wa", "tok", None),
        P("wa", "tok", None, None),
        P("wa", "tok", None),
        P("wa", "tok", None, None),
        P(None, "wa"),
        P(None, "wa"),
        P(None, "wa", None),
        P(None, "wa"),
        P(None, "wa", None),
        P(None, "wa"),
        P(None, "wa"),
        P(None, "wa"),
        P(None, "wa", None),
        P(None, "wa"),
        P(None, "wa", None),
        P(None, "wa"),
    )
    return jax.shard_map(local, mesh=mesh, in_specs=in_specs, out_specs=out_specs, check_vma=False)
```

```python
import functools

import jax
import jax.numpy as jnp
from jax import lax
from jax.experimental import pallas as pl
from jax.experimental.pallas import tpu as pltpu
from jax.sharding import PartitionSpec as P

HEAD = 64
PAIR = 2 * HEAD
LAYERS = 2
EPSILON = 1e-05
NEGATIVE = -1e30
CURVE = 0.7978845608028654
CUBIC = 0.044715
F32 = jnp.float32
BF16 = jnp.bfloat16

V_FG, V_FS, V_QKV, V_MB, V_SG, V_SS, V_RB, V_EB = 0, 1, 2, 5, 6, 7, 8, 9


def dot(left, right):
    return jnp.dot(left, right, preferred_element_type=F32)


def dot_nt(left, right):
    return lax.dot_general(left, right, (((1,), (1,)), ((), ())), preferred_element_type=F32)


def dot_tn(left, right):
    return lax.dot_general(left, right, (((0,), (0,)), ((), ())), preferred_element_type=F32)


def params(semantics=("arbitrary",), mib=56):
    return pltpu.CompilerParams(dimension_semantics=semantics, vmem_limit_bytes=mib * 2**20)


def cost(flops, nbytes, trans=0):
    return pl.CostEstimate(flops=int(flops), bytes_accessed=int(nbytes), transcendentals=int(trans))


def center(rows):
    centred = rows - jnp.mean(rows, -1, keepdims=True)
    inverse = lax.rsqrt(jnp.mean(centred * centred, -1, keepdims=True) + EPSILON)
    return centred * inverse, inverse


def norm_pull(rows, gain, grad):
    normal, inverse = center(rows)
    inner = grad * gain
    term = inverse * (
        inner
        - jnp.mean(inner, -1, keepdims=True)
        - normal * jnp.mean(inner * normal, -1, keepdims=True)
    )
    return term, jnp.sum(grad * normal, 0, keepdims=True), jnp.sum(grad, 0, keepdims=True)


def whole(shape):
    return pl.BlockSpec(shape, lambda *_: (0,) * len(shape))


def vector(width, place):
    return pl.BlockSpec((1, width), lambda *_: (0, place))


def qkv_kernel(x_ref, gain_ref, shift_ref, bias_ref, w_ref, out_ref, normed_ref):
    @pl.when(pl.program_id(0) == 0)
    def _():
        normal, _ = center(x_ref[...])
        normed_ref[...] = (normal * gain_ref[...] + shift_ref[...]).astype(BF16)

    out_ref[...] = (dot(normed_ref[...], w_ref[...]) + bias_ref[...]).astype(BF16)


def qkv_forward(stream, vec, weights, place):
    rows, width = stream.shape
    block = 512
    steps = 3 * width // block
    return pl.pallas_call(
        qkv_kernel,
        grid=(steps,),
        in_specs=[
            whole((rows, width)),
            vector(width, V_FG),
            vector(width, V_FS),
            pl.BlockSpec((1, block), lambda j: (0, V_QKV * width // block + j)),
            pl.BlockSpec((width, block), lambda j: (0, place // block + j)),
        ],
        out_specs=[pl.BlockSpec((rows, block), lambda j: (0, j)), whole((rows, width))],
        out_shape=[
            jax.ShapeDtypeStruct((rows, 3 * width), BF16),
            jax.ShapeDtypeStruct((rows, width), BF16),
        ],
        compiler_params=params(),
        cost_estimate=cost(6 * rows * width * width, 16 * 2**20),
        name="qkv_forward",
    )(stream, vec, vec, vec, weights)


def offsets(rows):
    return lax.broadcasted_iota(jnp.int32, (rows, rows), 0) - lax.broadcasted_iota(
        jnp.int32, (rows, rows), 1
    )


def head_lanes(block, half):
    lanes = lax.broadcasted_iota(jnp.int32, block.shape, 1) // HEAD
    return jnp.where(lanes == half, block, jnp.zeros_like(block))


def attend_kernel(pb, far, *refs):
    thr_ref, q_ref, k_ref, v_ref = refs[:4]
    far_refs = refs[4 : 4 + far]
    out_ref, lse_ref = refs[4 + far :]
    steps = offsets(pb)
    keys = [k_ref[:pb, :]] + [ref[0] for ref in far_refs]
    values = [v_ref[:pb, :]] + [ref[1] for ref in far_refs]
    total = None
    for half in range(2):
        q = head_lanes(q_ref[...], half) * jnp.asarray(HEAD**-0.5, BF16)
        lefts, rights = [], []
        for j, k in enumerate(keys):
            s = dot_nt(k, q)
            lefts.append(jnp.where(steps <= thr_ref[j], s[:, :pb], NEGATIVE))
            rights.append(s[:, pb:])
        own = jnp.where(steps <= 0, dot_nt(k_ref[pb:, :], q[pb:, :]), NEGATIVE)
        top_p = jnp.max(functools.reduce(jnp.maximum, lefts), 0, keepdims=True)
        top_c = jnp.max(functools.reduce(jnp.maximum, rights + [own]), 0, keepdims=True)
        sum_p = jnp.zeros((1, pb), F32)
        own = jnp.exp(own - top_c)
        sum_c = jnp.sum(own, 0, keepdims=True)
        acc_p = jnp.zeros((PAIR, pb), F32)
        acc_c = dot_tn(head_lanes(v_ref[pb:, :], half), own.astype(BF16))
        for j, v in enumerate(values):
            v = head_lanes(v, half)
            left = jnp.exp(lefts[j] - top_p)
            right = jnp.exp(rights[j] - top_c)
            sum_p += jnp.sum(left, 0, keepdims=True)
            sum_c += jnp.sum(right, 0, keepdims=True)
            acc_p += dot_tn(v, left.astype(BF16))
            acc_c += dot_tn(v, right.astype(BF16))
        lse_ref[half, :, :] = jnp.concatenate(
            [top_p + jnp.log(sum_p), top_c + jnp.log(sum_c)], 1
        )
        part = jnp.concatenate([acc_p / sum_p, acc_c / sum_c], 1)
        total = part if total is None else total + part
    out_ref[...] = total.T.astype(BF16)


def attend_forward(thr, qkv, far, part, parts):
    rows, width = qkv.shape[0], qkv.shape[1] // 3
    pb = rows // 2
    pairs = width // PAIR // parts
    place = lambda kind: pl.BlockSpec((rows, PAIR), lambda i: (0, (kind * parts + part) * pairs + i))
    block = pl.BlockSpec((2, pb, PAIR), lambda i: (0, 0, i))
    return pl.pallas_call(
        functools.partial(attend_kernel, pb, len(far)),
        grid=(pairs,),
        in_specs=[pl.BlockSpec(memory_space=pltpu.SMEM), place(0), place(1), place(2)]
        + [block] * len(far),
        out_specs=[
            pl.BlockSpec((rows, PAIR), lambda i: (0, i)),
            pl.BlockSpec((2, 1, rows), lambda i: (i, 0, 0)),
        ],
        out_shape=[
            jax.ShapeDtypeStruct((rows, width // parts), BF16),
            jax.ShapeDtypeStruct((2 * pairs, 1, rows), F32),
        ],
        compiler_params=params(),
        cost_estimate=cost(
            48 * rows * (len(far) + 2) * pb * width // parts,
            10 * 2**20 // parts,
            rows * (len(far) + 1) * pb * 16 // parts,
        ),
        name="attend_forward",
    )(thr, qkv, qkv, qkv, *far)


def attend_pull_kernel(pb, far, *refs):
    thr_ref, q_ref, k_ref, v_ref = refs[:4]
    far_refs = refs[4 : 4 + far]
    lse_ref, do_ref, o_ref = refs[4 + far : 7 + far]
    dq_ref, dcont_ref = refs[7 + far : 9 + far]
    dfar_refs = refs[9 + far :]
    steps = offsets(pb)
    scale = HEAD**-0.5
    keys = [k_ref[:pb, :]] + [ref[0] for ref in far_refs]
    values = [v_ref[:pb, :]] + [ref[1] for ref in far_refs]
    both = (do_ref[...].astype(F32) * o_ref[...].astype(F32)).T
    dq = jnp.zeros((PAIR, 2 * pb), F32)
    dks = [jnp.zeros((pb, PAIR), F32) for _ in keys]
    dvs = [jnp.zeros((pb, PAIR), F32) for _ in keys]
    dkc = jnp.zeros((pb, PAIR), F32)
    dvc = jnp.zeros((pb, PAIR), F32)
    dqc = jnp.zeros((PAIR, pb), F32)
    for half in range(2):
        q = head_lanes(q_ref[...], half) * jnp.asarray(scale, BF16)
        do = head_lanes(do_ref[...], half)
        lse = lse_ref[half, :, :]
        delta = jnp.sum(both[half * HEAD : (half + 1) * HEAD, :], 0, keepdims=True)
        for j, (k, v) in enumerate(zip(keys, values)):
            s = dot_nt(k, q)
            left = jnp.where(steps <= thr_ref[j], s[:, :pb], NEGATIVE)
            p = jnp.exp(jnp.concatenate([left, s[:, pb:]], 1) - lse)
            dp = dot_nt(v, do)
            ds = (p * (dp - delta)).astype(BF16)
            dvs[j] += dot(p.astype(BF16), do)
            dks[j] += dot(ds, q)
            dq += dot_tn(head_lanes(k, half), ds)
        kc, vc = k_ref[pb:, :], v_ref[pb:, :]
        s = jnp.where(steps <= 0, dot_nt(kc, q[pb:, :]), NEGATIVE)
        p = jnp.exp(s - lse[:, pb:])
        dp = dot_nt(vc, do[pb:, :])
        ds = (p * (dp - delta[:, pb:])).astype(BF16)
        dvc += dot(p.astype(BF16), do[pb:, :])
        dkc += dot(ds, q[pb:, :])
        dqc += dot_tn(head_lanes(kc, half), ds)
    for ref, dk, dv in zip(dfar_refs, dks, dvs):
        ref[0] = dk.astype(BF16)
        ref[1] = dv.astype(BF16)
    dcont_ref[0] = dkc.astype(BF16)
    dcont_ref[1] = dvc.astype(BF16)
    dq = jnp.concatenate([dq[:, :pb], dq[:, pb:] + dqc], 1)
    dq_ref[...] = (dq.T * scale).astype(BF16)


def attend_backward(thr, qkv, far, lse, do, attended, part, parts):
    rows, width = qkv.shape[0], qkv.shape[1] // 3
    pb = rows // 2
    pairs = width // PAIR // parts
    place = lambda kind: pl.BlockSpec((rows, PAIR), lambda i: (0, (kind * parts + part) * pairs + i))
    block = pl.BlockSpec((2, pb, PAIR), lambda i: (0, 0, i))
    column = pl.BlockSpec((rows, PAIR), lambda i: (0, i))
    pieces = len(far) + 2
    return pl.pallas_call(
        functools.partial(attend_pull_kernel, pb, len(far)),
        grid=(pairs,),
        in_specs=[pl.BlockSpec(memory_space=pltpu.SMEM), place(0), place(1), place(2)]
        + [block] * len(far)
        + [pl.BlockSpec((2, 1, rows), lambda i: (i, 0, 0)), place(0), column],
        out_specs=[column] + [block] * pieces,
        out_shape=[jax.ShapeDtypeStruct((rows, width // parts), BF16)]
        + [jax.ShapeDtypeStruct((2, pb, width // parts), BF16)] * pieces,
        compiler_params=params(),
        cost_estimate=cost(
            80 * rows * pieces * pb * width // parts,
            18 * 2**20 // parts,
            rows * pieces * pb * 16 // parts,
        ),
        name="attend_backward",
    )(thr, qkv, qkv, qkv, *far, lse, do, attended)


SLABS = 4
EARLY = 3


def feed_kernel(parts, x_ref, *refs):
    att_refs = refs[:parts]
    (wm_ref, mb_ref, gain_ref, shift_ref, eb_ref, rb_ref, w_ref,
     out_ref, middle_ref, second_ref, hidden_ref) = refs[parts:]
    width = x_ref.shape[1]

    @pl.when(pl.program_id(0) == 0)
    def _():
        middle = x_ref[...] + mb_ref[...]
        size = att_refs[0].shape[1]
        for part, ref in enumerate(att_refs):
            middle += dot(ref[...], wm_ref[part * size : (part + 1) * size, :])
        middle_ref[...] = middle
        normal, _ = center(middle)
        second_ref[...] = (normal * gain_ref[...] + shift_ref[...]).astype(BF16)
        out_ref[...] = middle + rb_ref[...]

    cut = width // 2
    for start in range(0, width, cut):
        hidden = dot(second_ref[...], w_ref[:, start : start + cut]) + eb_ref[:, start : start + cut]
        hidden_ref[:, start : start + cut] = hidden.astype(BF16)
        active = 0.5 * hidden * (1.0 + jnp.tanh(CURVE * hidden * (1.0 + CUBIC * hidden * hidden)))
        out_ref[...] += dot(active.astype(BF16), w_ref[start : start + cut, width:])


def feed_forward(stream, attended, vec, weights):
    rows, width = stream.shape
    array, at, mix_at = weights
    return pl.pallas_call(
        functools.partial(feed_kernel, len(attended)),
        grid=(SLABS,),
        in_specs=[whole((rows, width))]
        + [whole(piece.shape) for piece in attended]
        + [
            pl.BlockSpec((width, width), lambda j: (0, mix_at // width)),
            vector(width, V_MB),
            vector(width, V_SG),
            vector(width, V_SS),
            pl.BlockSpec((1, width), lambda j: (0, V_EB + j)),
            vector(width, V_RB),
            pl.BlockSpec((width, 2 * width), lambda j: (0, at // (2 * width) + j)),
        ],
        out_specs=[
            whole((rows, width)),
            whole((rows, width)),
            whole((rows, width)),
            pl.BlockSpec((rows, width), lambda j: (0, j)),
        ],
        out_shape=[
            jax.ShapeDtypeStruct((rows, width), F32),
            jax.ShapeDtypeStruct((rows, width), F32),
            jax.ShapeDtypeStruct((rows, width), BF16),
            jax.ShapeDtypeStruct((rows, SLABS * width), BF16),
        ],
        compiler_params=params(),
        cost_estimate=cost(18 * rows * width * width, 30 * 2**20, rows * SLABS * width),
        name="feed_forward",
    )(stream, *attended, array, vec, vec, vec, vec, vec, array)


def put_rows(refs, grad, core):
    if len(refs) == 1:
        refs[0][...] = grad
        return
    mine, other = refs
    planes, span, block = mine.shape
    split = grad.reshape(planes, 2, span, block)
    first = core == 0
    mine[...] = jnp.where(first, split[:, 0], split[:, 1])
    other[...] = jnp.where(first, split[:, 1], split[:, 0])


def grad_outs(holders, width, columns, block, apart):
    if not apart:
        return [pl.BlockSpec((width, block), lambda j: (0, j))], [
            jax.ShapeDtypeStruct((width, columns), BF16)
        ]
    shape = (holders // 2, width // holders)
    spec = pl.BlockSpec(shape + (block,), lambda j: (0, 0, j))
    return [spec] * 2, [jax.ShapeDtypeStruct(shape + (columns,), BF16)] * 2


def feed_pull_kernel(final, slabs, parts, outs, core_ref, gs_ref, *refs):
    att_refs, refs = refs[:parts], refs[parts:]
    hidden_ref, second_ref, w_ref = refs[:3]
    refs = refs[3:]
    if final:
        middle_ref, gain_ref, wm_ref, before_ref = refs[:4]
        refs = refs[4:]
    dw_refs, deb_ref, refs = refs[:outs], refs[outs], refs[outs + 1 :]
    if final:
        gm_ref, gatt_ref, dsg_ref, dss_ref, dmb_ref, acc_ref = refs[:6]
    else:
        acc_ref, drb_ref = refs[:2]
    gb_scr, sec_scr, act_scr = refs[-3:]
    step = pl.program_id(0)
    core = core_ref[0]
    width = gs_ref.shape[1]

    @pl.when(step == 0)
    def _():
        branch = gs_ref[...].astype(BF16)
        gb_scr[...] = branch
        sec_scr[...] = second_ref[...].T
        if final:
            acc_ref[...] = before_ref[...]
        else:
            acc_ref[...] = jnp.zeros_like(acc_ref)
            drb_ref[...] = jnp.sum(branch.astype(F32), 0, keepdims=True)

    @pl.when((step % 2 == 0) & (step < 2 * slabs))
    def _():
        cut = width // 2
        for start in range(0, width, cut):
            columns = slice(start, start + cut)
            grad_active = dot_nt(gb_scr[...], w_ref[columns, width:])
            v = hidden_ref[:, columns].astype(F32)
            square = v * v
            t = jnp.tanh(CURVE * v * (1.0 + CUBIC * square))
            half = 0.5 + 0.5 * t
            slope = half + 0.5 * v * (1.0 - t * t) * (CURVE * (1.0 + 3 * CUBIC * square))
            grad_hidden = (grad_active * slope).astype(BF16)
            act_scr[:, columns] = (v * half).astype(BF16)
            deb_ref[:, columns] = jnp.sum(grad_hidden.astype(F32), 0, keepdims=True)
            acc_ref[...] += dot_nt(grad_hidden, w_ref[:, columns])
            put_rows(
                [ref.at[..., columns] for ref in dw_refs],
                dot(sec_scr[...], grad_hidden).astype(BF16),
                core,
            )

    @pl.when(step % 2 == 1)
    def _():
        put_rows(dw_refs, dot_tn(act_scr[...], gb_scr[...]).astype(BF16), core)

    if not final:
        return

    @pl.when(step == 2 * slabs)
    def _():
        term, dgain, dshift = norm_pull(middle_ref[...], gain_ref[...], acc_ref[...])
        dsg_ref[...] = dgain
        dss_ref[...] = dshift
        grad_middle = gs_ref[...] + term
        gm_ref[...] = grad_middle
        grad_mix = grad_middle.astype(BF16)
        dmb_ref[...] = jnp.sum(grad_mix.astype(F32), 0, keepdims=True)
        gatt_ref[...] = dot_nt(grad_mix, wm_ref[...]).astype(BF16)
        size = att_refs[0].shape[1]
        for part, ref in enumerate(att_refs):
            sec_scr[part * size : (part + 1) * size, :] = ref[...].T
        put_rows(dw_refs, dot(sec_scr[...], grad_mix).astype(BF16), core)


def feed_backward(holders, core, grad_stream, hidden, second, vec, weights, apart, final=()):
    rows, width = grad_stream.shape
    array, at, mix_at = weights
    half = SLABS - EARLY if final else EARLY
    row = whole((1, width))
    small = jax.ShapeDtypeStruct((1, width), F32)
    base = EARLY if final else 0
    slab = lambda j: base + jnp.minimum(j // 2, half - 1)
    blocks = 2 * half + 1 if final else 2 * half
    dw_specs, dw_shapes = grad_outs(holders, width, blocks * width, width, apart)
    square = whole((rows, width))
    in_specs = [
        pl.BlockSpec((rows, width), lambda j: (0, slab(j))),
        square,
        pl.BlockSpec((width, 2 * width), lambda j: (0, at // (2 * width) + slab(j))),
    ]
    operands = [hidden, second, array]
    out_specs = dw_specs + [pl.BlockSpec((1, width), lambda j: (0, slab(j) - base))]
    out_shape = dw_shapes + [jax.ShapeDtypeStruct((1, half * width), F32)]
    total = jax.ShapeDtypeStruct((rows, width), F32)
    scratch = [
        pltpu.VMEM((rows, width), BF16),
        pltpu.VMEM((width, rows), BF16),
        pltpu.VMEM((rows, width), BF16),
    ]
    attended = []
    if final:
        middle, attended, so_far = final
        in_specs += [
            square,
            vector(width, V_SG),
            pl.BlockSpec((width, width), lambda j: (0, mix_at // width)),
            square,
        ]
        operands += [middle, vec, array, so_far]
        out_specs += [square, square, row, row, row]
        out_shape += [total, jax.ShapeDtypeStruct((rows, width), BF16), small, small, small]
        scratch = [pltpu.VMEM((rows, width), F32)] + scratch
    else:
        out_specs += [square, row]
        out_shape += [total, small]
    return pl.pallas_call(
        functools.partial(feed_pull_kernel, bool(final), half, len(attended), len(dw_specs)),
        grid=(blocks,),
        in_specs=[pl.BlockSpec(memory_space=pltpu.SMEM), square]
        + [whole(piece.shape) for piece in attended]
        + in_specs,
        out_specs=out_specs,
        out_shape=out_shape,
        scratch_shapes=scratch,
        compiler_params=params(),
        cost_estimate=cost(blocks * 4 * rows * width * width, blocks * 5 * 2**20, rows * half * width),
        name="feed_backward",
    )(core, grad_stream, *attended, *operands)


def qkv_pull_kernel(parts, sums, outs, core_ref, *refs):
    dq_refs, refs = refs[:parts], refs[parts:]
    cont_refs, refs = refs[:parts], refs[parts:]
    sum_refs, refs = refs[: parts * sums], refs[parts * sums :]
    normed_ref, x_ref, gm_ref, gain_ref, w_ref = refs[:5]
    dw_refs = refs[5 : 5 + outs]
    out_ref, dbias_ref, dgain_ref, dshift_ref, norm_scr, acc_scr, g_scr = refs[5 + outs :]
    step = pl.program_id(0)

    @pl.when(step == 0)
    def _():
        norm_scr[...] = normed_ref[...].T
        acc_scr[...] = jnp.zeros_like(acc_scr)
        for part in range(parts):
            g_scr[part] = dq_refs[part][...]
            total = sum(ref[...].astype(F32) for ref in sum_refs[part * sums : (part + 1) * sums])
            for kind in range(2):
                both = jnp.concatenate([total[kind].astype(BF16), cont_refs[part][kind]], 0)
                g_scr[(1 + kind) * parts + part] = both

    grad = g_scr[step]
    dbias_ref[...] = jnp.sum(grad.astype(F32), 0, keepdims=True)
    put_rows(dw_refs, dot(norm_scr[...], grad).astype(BF16), core_ref[0])
    acc_scr[...] += dot_nt(grad, w_ref[...])

    @pl.when(step == pl.num_programs(0) - 1)
    def _():
        term, dgain, dshift = norm_pull(x_ref[...], gain_ref[...], acc_scr[...])
        dgain_ref[...] = dgain
        dshift_ref[...] = dshift
        out_ref[...] = gm_ref[...] + term


def qkv_backward(holders, core, dqs, conts, sums, normed, stream, grad_middle, vec, weights):
    rows, width = stream.shape
    parts = len(dqs)
    block = width // parts
    wq, place = weights
    small = jax.ShapeDtypeStruct((1, width), F32)
    flat = [piece for part in sums for piece in part]
    dw_specs, dw_shapes = grad_outs(holders, width, 3 * width, block, True)
    return pl.pallas_call(
        functools.partial(qkv_pull_kernel, parts, len(sums[0]), len(dw_specs)),
        grid=(3 * parts,),
        in_specs=[pl.BlockSpec(memory_space=pltpu.SMEM)]
        + [whole(piece.shape) for piece in dqs + conts + flat]
        + [
            whole((rows, width)),
            whole((rows, width)),
            whole((rows, width)),
            vector(width, V_FG),
            pl.BlockSpec((width, block), lambda j: (0, place // block + j)),
        ],
        out_specs=dw_specs
        + [
            whole((rows, width)),
            pl.BlockSpec((1, block), lambda j: (0, j)),
            whole((1, width)),
            whole((1, width)),
        ],
        out_shape=dw_shapes
        + [
            jax.ShapeDtypeStruct((rows, width), F32),
            jax.ShapeDtypeStruct((1, 3 * width), F32),
            small,
            small,
        ],
        scratch_shapes=[
            pltpu.VMEM((width, rows), BF16),
            pltpu.VMEM((rows, width), F32),
            pltpu.VMEM((3 * parts, rows, block), BF16),
        ],
        compiler_params=params(),
        cost_estimate=cost(12 * rows * width * width, 24 * 2**20),
        name="qkv_backward",
    )(core, *dqs, *conts, *flat, normed, stream, grad_middle, vec, wq)


def trade(block, axis, bits):
    return lax.ppermute(block, axis, [(i, i ^ bits) for i in range(lax.axis_size(axis))])


def pick(block, place, axis):
    return lax.dynamic_index_in_dim(block, place, axis, keepdims=False)


def added(*blocks):
    return sum(block.astype(F32) for block in blocks).astype(BF16)


def split_kernel(count, lows, bits_ref, *refs):
    for side, low in enumerate(lows):
        ins = refs[side * count : (side + 1) * count]
        keep_ref, send_ref = refs[2 * count + 2 * side : 2 * count + 2 * side + 2]
        bit = bits_ref[side]
        for k in range(keep_ref.shape[1]):
            base = (k >> low << (low + 1)) | (k & ((1 << low) - 1))
            for ref, value in ((keep_ref, bit), (send_ref, 1 - bit)):
                place = base + (value << low)
                ref[:, k] = sum(one[:, place].astype(F32) for one in ins).astype(BF16)


def split_sum(sides, bits, lows, starts, cut):
    planes, holders, share, _ = sides[0][0].shape
    piece = next(size for size in range(cut, 0, -128) if all(start % size == 0 for start in starts))
    deep = max(1, planes // 2)
    specs = [
        pl.BlockSpec((deep, holders, share, piece), lambda i, j, start=start: (i, 0, 0, start // piece + j))
        for blocks, start in zip(sides, starts)
        for _ in blocks
    ]
    out = pl.BlockSpec((deep, holders // 2, share, piece), lambda i, j: (i, 0, 0, j))
    return pl.pallas_call(
        functools.partial(split_kernel, len(sides[0]), lows),
        grid=(planes // deep, cut // piece),
        in_specs=[pl.BlockSpec(memory_space=pltpu.SMEM)] + specs,
        out_specs=[out] * 4,
        out_shape=[jax.ShapeDtypeStruct((planes, holders // 2, share, cut), BF16)] * 4,
        compiler_params=params(("arbitrary",) * 2),
        cost_estimate=cost(planes * holders * share * cut * 4, 12 * planes * holders * share * cut),
        name="split_sum",
    )(jnp.stack(bits), *sides[0], *sides[1])


def plane_kernel(plane_ref, *refs):
    ins, outs = refs[:4], refs[4:]
    cut = ins[0].shape[-1]
    for step, ref in enumerate(outs):
        place = jnp.bitwise_xor(plane_ref[0], step)
        for side in range(2):
            value = ins[2 * side][place, 0].astype(F32) + ins[2 * side + 1][place, 0].astype(F32)
            ref[:, side * cut : (side + 1) * cut] = value.astype(BF16)


def plane_rows(blocks, plane):
    planes, _, share, cut = blocks[0].shape
    return pl.pallas_call(
        plane_kernel,
        grid=(1,),
        in_specs=[pl.BlockSpec(memory_space=pltpu.SMEM)] + [whole(block.shape) for block in blocks],
        out_specs=[whole((share, 2 * cut))] * planes,
        out_shape=[jax.ShapeDtypeStruct((share, 2 * cut), BF16)] * planes,
        compiler_params=params(),
        cost_estimate=cost(planes * share * cut * 4, planes * share * cut * 12),
        name="plane_rows",
    )(plane.reshape(1), *blocks)


def reduce_stages(*pairs):
    planes, span, columns = pairs[0][0].shape
    n_tok = lax.axis_size("tok")
    me, plane = lax.axis_index("tok"), lax.axis_index("wa") // 2
    bits = n_tok.bit_length() - 1
    cut = columns * len(pairs) // 2
    sides = [
        [
            block.reshape(planes, n_tok, span // n_tok, columns)
            for block in (mine, trade(other, "wa", 1))
        ]
        for mine, other in pairs
    ]
    starts = [0, 0]
    if len(pairs) == 1:
        sides, starts = sides * 2, [0, cut]
    orders = [list(range(bits)), list(reversed(range(bits)))]
    left = [list(range(bits)), list(range(bits))]
    for turn in range(bits):
        lows = []
        for order, rest in zip(orders, left):
            lows.append(rest.index(order[turn]))
            rest.remove(order[turn])
        own = [(me >> order[turn]) & 1 for order in orders]
        keep0, send0, keep1, send1 = split_sum(sides, own, lows, starts, cut)
        starts = [0, 0]
        sends = yield [send0, send1]
        sides = [
            [keep, trade(send, "tok", 1 << order[turn])]
            for keep, send, order in zip((keep0, keep1), sends, orders)
        ]
    sends = plane_rows(sides[0] + sides[1], plane)
    sends = yield sends
    got = [trade(send, "wa", 2 * step) for step, send in enumerate(sends) if step]
    return added(sends[0], *got)


def assemble_kernel(planes, holders, places_ref, *refs):
    own_ref, sibling_ref = refs[:2]
    near_refs, far_refs = refs[2 : 2 + holders], refs[2 + holders : 2 + 2 * holders]
    out_ref, sems = refs[-2:]
    wa, me = places_ref[0], places_ref[1]
    copies = []

    def copy(source, target):
        copies.append(pltpu.make_async_copy(source, target, sems.at[len(copies)]))
        copies[-1].start()

    copy(own_ref, out_ref.at[wa])
    copy(sibling_ref, out_ref.at[jnp.bitwise_xor(wa, 1)])
    for core, group in enumerate((near_refs, far_refs)):
        for turn, ref in enumerate(group):
            for step in range(1, planes):
                place = out_ref.at[jnp.bitwise_xor(wa, 2 * step + core), jnp.bitwise_xor(me, turn)]
                copy(ref.at[step - 1], place)
    for one in copies:
        one.wait()


def assemble(own, sibling, near, far):
    holders, share, columns = own.shape
    planes = near[0].shape[0] + 1
    anywhere = pl.BlockSpec(memory_space=pl.ANY)
    places = jnp.stack([lax.axis_index("wa"), lax.axis_index("tok")])
    whole_array = pl.pallas_call(
        functools.partial(assemble_kernel, planes, holders),
        in_specs=[pl.BlockSpec(memory_space=pltpu.SMEM)] + [anywhere] * (2 + 2 * holders),
        out_specs=anywhere,
        out_shape=jax.ShapeDtypeStruct((2 * planes, holders, share, columns), BF16),
        scratch_shapes=[pltpu.SemaphoreType.DMA((2 + 2 * holders * (planes - 1),))],
        compiler_params=pltpu.CompilerParams(vmem_limit_bytes=2**22),
        cost_estimate=cost(0, 8 * planes * holders * share * columns),
        name="assemble",
    )(places, own, sibling, *near, *far)
    return whole_array.reshape(-1, columns)


class Gathering:
    def __init__(self, shard):
        n_tok = lax.axis_size("tok")
        self.own = shard.reshape(n_tok, -1, shard.shape[1])
        self.ready = pick(self.own, lax.axis_index("tok"), 0)
        self.stage = 0

    def go(self, ready):
        planes, n_tok = lax.axis_size("wa") // 2, lax.axis_size("tok")
        if self.stage == 0:
            self.sibling = trade(self.own, "wa", 1)
            self.ready = jnp.stack([trade(ready, "wa", 2 * step) for step in range(1, planes)])
        elif self.stage == 1:
            self.near = [ready] + [trade(ready, "tok", step) for step in range(1, n_tok)]
            self.far = [trade(ready, "wa", 1)]
            self.ready = self.near
        elif self.stage == 2:
            self.near = ready
            self.far += [trade(block, "wa", 1) for block in ready[1:]]
            self.ready = None
        self.stage += 1

    def finish(self):
        while self.ready is not None:
            self.go(self.ready)
        return assemble(self.own, self.sibling, self.near, self.far)


def pack_kernel(span, me_ref, expand_ref, reduce_ref, mix_ref, qkv_ref, *out_refs):
    del me_ref
    width = mix_ref.shape[2]
    wide = (2 * SLABS + 1) * width
    for layer, out_ref in enumerate(out_refs):
        for a in range(SLABS):
            start = 2 * a * width
            for w in range(width // span):
                place = (w * SLABS + a) * span
                piece = expand_ref[layer, :, place : place + span]
                out_ref[:, start + w * span : start + (w + 1) * span] = piece
            out_ref[:, start + width : start + 2 * width] = reduce_ref[layer, a, 0]
        out_ref[:, wide - width : wide] = mix_ref[layer]
        if not layer:
            out_ref[:, wide:] = qkv_ref[1]


def pack(expand, reduce, mix, qkv):
    n_tok, me = lax.axis_size("tok"), lax.axis_index("tok")
    layers, span, width = mix.shape
    share = span // n_tok
    wide = (2 * SLABS + 1) * width
    by_row = lambda size: pl.BlockSpec((layers, share, size), lambda i, me: (0, me[0], 0))
    shapes = [(share, wide + 3 * width), (share, wide)]
    return pl.pallas_call(
        functools.partial(pack_kernel, span),
        grid_spec=pltpu.PrefetchScalarGridSpec(
            num_scalar_prefetch=1,
            grid=(1,),
            in_specs=[
                by_row(SLABS * width),
                pl.BlockSpec((layers, SLABS, 1, share, width), lambda i, me: (0, 0, me[0], 0, 0)),
                by_row(width),
                by_row(3 * width),
            ],
            out_specs=[pl.BlockSpec(shape, lambda i, me: (0, 0)) for shape in shapes],
        ),
        out_shape=[jax.ShapeDtypeStruct(shape, BF16) for shape in shapes],
        compiler_params=params(),
        cost_estimate=cost(0, 8 * share * wide),
        name="pack",
    )(
        me.reshape(1), expand, reduce.reshape(layers, SLABS, n_tok, share, width), mix, qkv
    )


class Reduction:
    def __init__(self, *pairs):
        self.walk = reduce_stages(*pairs)
        self.result = None
        self.ready = next(self.walk)

    def go(self, values):
        try:
            self.ready = self.walk.send(values)
        except StopIteration as stop:
            self.ready = None
            self.result = stop.value

    def finish(self):
        while self.ready is not None:
            self.go(self.ready)
        return self.result


def together(value, reductions):
    active = [item for item in reductions if item.ready is not None]
    value, ready = lax.optimization_barrier((value, [item.ready for item in active]))
    for item, values in zip(active, ready):
        item.go(values)
    return value


def feed_out_kernel(pieces, me_ref, *refs):
    mix_ref, expand_ref, reduce_ref = refs[-3:]
    span, width = mix_ref.shape[1] * mix_ref.shape[2], mix_ref.shape[3]
    for step, ref in enumerate(refs[:pieces]):
        place = jnp.bitwise_xor(me_ref[0], step)
        for a in range(SLABS):
            for w in range(width // span):
                there = 2 * a * width + w * span
                value = ref[:, there : there + span].astype(F32)
                expand_ref[0, place, :, (w * SLABS + a) * span : (w * SLABS + a + 1) * span] = value
            there = (2 * a + 1) * width
            reduce_ref[0, a, place] = ref[:, there : there + width].astype(F32)
        mix_ref[0, place] = ref[:, 2 * SLABS * width :].astype(F32)


def feed_out(pieces, width, me, layer, held):
    n_tok = len(pieces)
    share = pieces[0].shape[0]
    shapes = [(n_tok, share, width), (n_tok, share, SLABS * width), (SLABS, n_tok, share, width)]
    return pl.pallas_call(
        functools.partial(feed_out_kernel, n_tok),
        grid=(1,),
        in_specs=[pl.BlockSpec(memory_space=pltpu.SMEM)]
        + [whole((share, (2 * SLABS + 1) * width)) for _ in pieces]
        + [pl.BlockSpec(memory_space=pl.ANY) for _ in held],
        out_specs=[
            pl.BlockSpec((1,) + shape, lambda i, rank=len(shape): (layer,) + (0,) * rank)
            for shape in shapes
        ],
        out_shape=[jax.ShapeDtypeStruct((LAYERS,) + shape, F32) for shape in shapes],
        input_output_aliases={1 + n_tok + k: k for k in range(len(held))},
        compiler_params=params(),
        cost_estimate=cost(9 * share * n_tok * width, 6 * 9 * share * n_tok * width),
        name="feed_out",
    )(me.reshape(1), *pieces, *held)


def qkv_out_kernel(pieces, me_ref, *refs):
    out_ref = refs[-1]
    for step, ref in enumerate(refs[:pieces]):
        out_ref[0, jnp.bitwise_xor(me_ref[0], step)] = ref[...].astype(F32)


def qkv_out(pieces, columns, me, layer, held):
    share = pieces[0].shape[0]
    shape = (len(pieces), share, columns)
    last = pieces[0].shape[1] // columns - 1
    return pl.pallas_call(
        functools.partial(qkv_out_kernel, len(pieces)),
        grid=(1,),
        in_specs=[pl.BlockSpec(memory_space=pltpu.SMEM)]
        + [pl.BlockSpec((share, columns), lambda i: (0, last)) for _ in pieces]
        + [pl.BlockSpec(memory_space=pl.ANY) for _ in held],
        out_specs=pl.BlockSpec((1,) + shape, lambda i: (layer, 0, 0, 0)),
        out_shape=jax.ShapeDtypeStruct((LAYERS,) + shape, F32),
        input_output_aliases={1 + len(pieces) + k: k for k in range(len(held))},
        compiler_params=params(),
        cost_estimate=cost(share * columns, 24 * share * columns),
        name="qkv_out",
    )(me.reshape(1), *pieces, *held)


def local(
    prompt_in, cont_in, first_gain, first_shift, qkv_weight, qv_bias, mix_weight, mix_bias,
    second_gain, second_shift, expand_weight, expand_bias, reduce_weight, reduce_bias, owners,
    prompt_cot, cont_cot,
):
    n_tok, n_wa = lax.axis_size("tok"), lax.axis_size("wa")
    me = lax.axis_index("tok")
    core = (lax.axis_index("wa") % 2).reshape(1)
    rows = prompt_in.shape[1]
    width = prompt_in.shape[2]
    span = width // n_wa
    parts = 2
    steps = list(range(1, n_tok))
    order = owners[0]
    by_step = jnp.stack([pick(order, me ^ step, 0) for step in [0] + steps])
    thr = (by_step[0] - by_step) * rows

    small = jnp.concatenate(
        [first_gain, first_shift, qv_bias, mix_bias, second_gain, second_shift, reduce_bias, expand_bias], 1
    )
    small = lax.all_gather(small, "wa", axis=0, tiled=False)

    def spread(layer):
        def piece(start, count):
            return small[:, layer, start * span : (start + count) * span].reshape(1, -1)

        pair = piece(2, 2)
        units = small[:, layer, 8 * span : 12 * span].reshape(n_wa, SLABS, span)
        pieces = [
            piece(0, 1), piece(1, 1), pair[:, :width], jnp.zeros((1, width), BF16), pair[:, width:],
            piece(4, 1), piece(5, 1), piece(6, 1), piece(7, 1),
            units.transpose(1, 0, 2).reshape(1, SLABS * width),
        ]
        return jnp.concatenate(pieces, 1).astype(F32)

    vecs = [spread(layer) for layer in range(LAYERS)]
    both = ("wa", "tok")
    share = span // n_tok

    wide = (2 * SLABS + 1) * width
    first = Gathering(qkv_weight[0])
    rows_middle, rows_last = pack(expand_weight, reduce_weight, mix_weight, qkv_weight)
    middle_array = lax.all_gather(rows_middle, both, axis=0, tiled=True)
    last_array = lax.all_gather(rows_last, both, axis=0, tiled=True)
    first = first.finish()

    stream = jnp.concatenate([prompt_in[0], cont_in[0, 0]], 0).astype(F32)
    kept = []
    size = width // parts
    weights = [
        ((first, 0), (middle_array, 0, wide - width)),
        ((middle_array, wide), (last_array, 0, wide - width)),
    ]
    for layer in range(LAYERS):
        wq, wf = weights[layer]
        qkv, normed = qkv_forward(stream, vecs[layer], *wq)
        fars, attended, lses = [], [], []
        for part in range(parts):
            block = jnp.stack(
                [
                    qkv[:rows, kind * width + part * size : kind * width + (part + 1) * size]
                    for kind in (1, 2)
                ]
            )
            fars.append([trade(block, "tok", step) for step in steps])
        for part in range(parts):
            one, lse = attend_forward(thr, qkv, fars[part], part, parts)
            attended.append(one)
            lses.append(lse)
        result, middle, second, hidden = feed_forward(stream, attended, vecs[layer], wf)
        kept.append((stream, normed, qkv, fars, lses, attended, middle, second, hidden))
        stream = result

    grad_stream = jnp.concatenate([prompt_cot[0], cont_cot[0, 0]], 0).astype(F32)
    smalls = [None] * LAYERS
    sync = lax.optimization_barrier

    def spread_rows(block):
        block = block.reshape(n_tok, share, block.shape[1])
        return [pick(block, me ^ step, 0) for step in [0] + steps]

    def from_each(blocks):
        return [blocks[0]] + [trade(block, "tok", step) for step, block in zip(steps, blocks[1:])]

    def to_each(block):
        return from_each([block] * n_tok)

    late, last, early = [None] * LAYERS, [None] * LAYERS, [None] * LAYERS
    for layer in reversed(range(LAYERS)):
        wq, wf = weights[layer]
        start, normed, qkv, fars, lses, attended, middle, second, hidden = kept[layer]
        if not layer:
            grad_stream = together(grad_stream, [late[1]])
        common = (n_wa, core, grad_stream, hidden, second, vecs[layer], wf)
        dw_early, deb_low, so_far, drb = feed_backward(*common, False)
        early[layer] = lax.psum_scatter(dw_early, "wa", scatter_dimension=0, tiled=True)
        if not layer:
            so_far, spread = together((so_far, spread_rows(early[1])), [late[1], last[1]])
            early[1] = added(*from_each(spread))
        late_mine, late_other, deb_high, grad_middle, grad_att, dsg, dss, dmb = feed_backward(
            *common, True, (middle, attended, so_far)
        )
        dqs, conts, sums = [], [], []
        for part in range(parts):
            if not layer:
                grad_att = together(grad_att, [last[1]])
            if layer or part:
                late[layer] = late[layer] or Reduction((late_mine, late_other))
            dq, cont, own, *far = attend_backward(
                thr, qkv, fars[part], lses[part], grad_att, attended[part], part, parts
            )
            dqs.append(dq)
            conts.append(cont)
            sums.append([own] + [trade(block, "tok", step) for step, block in zip(steps, far)])
        conts[-1] = together(conts[-1], [late[layer]])
        if not layer:
            upper = jnp.concatenate([early[1], late[1].finish(), last[1].finish()], 1)
            conts[-1], upper = sync((conts[-1], upper))
            upper = to_each(upper)
        dwq_mine, dwq_other, grad_stream, dqb, dfg, dfs = qkv_backward(
            n_wa, core, dqs, conts, sums, normed, start, grad_middle, vecs[layer], wq
        )
        last[layer] = Reduction((dwq_mine, dwq_other))
        dqb = jnp.concatenate([dqb[:, :width], dqb[:, 2 * width :]], 1)
        deb = jnp.concatenate([deb_low, deb_high], 1)
        deb = deb.reshape(SLABS, n_wa, span).transpose(1, 0, 2)
        smalls[layer] = [
            piece.reshape(n_wa, -1) for piece in (dfg, dfs, dqb, dmb, dsg, dss, deb, drb)
        ]

    small = jnp.stack([jnp.concatenate(pieces, 1) for pieces in smalls], 1)
    bits = n_wa.bit_length() - 1
    small = small.reshape((2,) * bits + small.shape[1:])
    for bit in reversed(range(bits)):
        place = (lax.axis_index("wa") >> bit) & 1
        small = pick(small, place, 0) + trade(pick(small, 1 - place, 0), "wa", 1 << bit)
    for step in [1 << bit for bit in range(n_tok.bit_length() - 1)]:
        small = small + trade(small, "tok", step)

    spread = together(spread_rows(early[0]), [late[0], last[0]])
    early[0] = added(*from_each(spread))
    early[0] = together(early[0], [late[0], last[0]])
    lower = jnp.concatenate([early[0], late[0].finish()], 1)
    upper, lower = together((upper, lower), [last[0]])
    feeds = feed_out(upper, width, me, 1, [])
    qkvs = qkv_out(upper, 3 * width, me, 1, [])
    feeds = feed_out(to_each(lower), width, me, 0, feeds)
    qkvs = qkv_out(to_each(last[0].finish()), 3 * width, me, 0, [qkvs])
    mixes, expands, reduces = [
        block.reshape(LAYERS, -1, width) if place != 1 else block.reshape(LAYERS, span, -1)
        for place, block in enumerate(feeds)
    ]
    qkvs = qkvs.reshape(LAYERS, span, 3 * width)

    def vec_out(start, count):
        return small[:, start * span : (start + count) * span]

    return (
        stream[:rows][None],
        stream[rows:][None, None],
        grad_stream[:rows][None],
        grad_stream[rows:][None, None],
        vec_out(0, 1),
        vec_out(1, 1),
        qkvs,
        vec_out(2, 2),
        mixes,
        vec_out(4, 1),
        vec_out(5, 1),
        vec_out(6, 1),
        expands,
        vec_out(7, 4),
        reduces,
        vec_out(11, 1),
    )


def solution(mesh):
    in_specs = (
        P("wa", "tok", None),
        P("wa", "tok", None, None),
        P(None, "wa"),
        P(None, "wa"),
        P(None, "wa", None),
        P(None, "wa"),
        P(None, "wa", None),
        P(None, "wa"),
        P(None, "wa"),
        P(None, "wa"),
        P(None, "wa", None),
        P(None, "wa"),
        P(None, "wa", None),
        P(None, "wa"),
        P("wa", None),
        P("wa", "tok", None),
        P("wa", "tok", None, None),
    )
    out_specs = (
        P("wa", "tok", None),
        P("wa", "tok", None, None),
        P("wa", "tok", None),
        P("wa", "tok", None, None),
        P(None, "wa"),
        P(None, "wa"),
        P(None, "wa", None),
        P(None, "wa"),
        P(None, "wa", None),
        P(None, "wa"),
        P(None, "wa"),
        P(None, "wa"),
        P(None, "wa", None),
        P(None, "wa"),
        P(None, "wa", None),
        P(None, "wa"),
    )
    return jax.shard_map(local, mesh=mesh, in_specs=in_specs, out_specs=out_specs, check_vma=False)
```

```python
import functools

import jax
import jax.numpy as jnp
from jax import lax
from jax.experimental import pallas as pl
from jax.experimental.pallas import tpu as pltpu
from jax.sharding import PartitionSpec as P

HEAD = 64
PAIR = 2 * HEAD
LAYERS = 2
EPSILON = 1e-05
NEGATIVE = -1e30
CURVE = 0.7978845608028654
CUBIC = 0.044715
F32 = jnp.float32
BF16 = jnp.bfloat16

V_FG, V_FS, V_QKV, V_MB, V_SG, V_SS, V_RB, V_EB = 0, 1, 2, 5, 6, 7, 8, 9


def dot(left, right):
    return jnp.dot(left, right, preferred_element_type=F32)


def dot_nt(left, right):
    return lax.dot_general(left, right, (((1,), (1,)), ((), ())), preferred_element_type=F32)


def dot_tn(left, right):
    return lax.dot_general(left, right, (((0,), (0,)), ((), ())), preferred_element_type=F32)


def params(semantics=("arbitrary",), mib=56):
    return pltpu.CompilerParams(dimension_semantics=semantics, vmem_limit_bytes=mib * 2**20)


def cost(flops, nbytes, trans=0):
    return pl.CostEstimate(flops=int(flops), bytes_accessed=int(nbytes), transcendentals=int(trans))


def center(rows):
    centred = rows - jnp.mean(rows, -1, keepdims=True)
    inverse = lax.rsqrt(jnp.mean(centred * centred, -1, keepdims=True) + EPSILON)
    return centred * inverse, inverse


def norm_pull(rows, gain, grad):
    normal, inverse = center(rows)
    inner = grad * gain
    term = inverse * (
        inner
        - jnp.mean(inner, -1, keepdims=True)
        - normal * jnp.mean(inner * normal, -1, keepdims=True)
    )
    return term, jnp.sum(grad * normal, 0, keepdims=True), jnp.sum(grad, 0, keepdims=True)


def whole(shape):
    return pl.BlockSpec(shape, lambda *_: (0,) * len(shape))


def vector(width, place):
    return pl.BlockSpec((1, width), lambda *_: (0, place))


def qkv_kernel(x_ref, gain_ref, shift_ref, bias_ref, w_ref, out_ref, normed_ref):
    @pl.when(pl.program_id(0) == 0)
    def _():
        normal, _ = center(x_ref[...])
        normed_ref[...] = (normal * gain_ref[...] + shift_ref[...]).astype(BF16)

    out_ref[...] = (dot(normed_ref[...], w_ref[...]) + bias_ref[...]).astype(BF16)


def qkv_forward(stream, vec, weights, place):
    rows, width = stream.shape
    block = 512
    steps = 3 * width // block
    return pl.pallas_call(
        qkv_kernel,
        grid=(steps,),
        in_specs=[
            whole((rows, width)),
            vector(width, V_FG),
            vector(width, V_FS),
            pl.BlockSpec((1, block), lambda j: (0, V_QKV * width // block + j)),
            pl.BlockSpec((width, block), lambda j: (0, place // block + j)),
        ],
        out_specs=[pl.BlockSpec((rows, block), lambda j: (0, j)), whole((rows, width))],
        out_shape=[
            jax.ShapeDtypeStruct((rows, 3 * width), BF16),
            jax.ShapeDtypeStruct((rows, width), BF16),
        ],
        compiler_params=params(),
        cost_estimate=cost(6 * rows * width * width, 16 * 2**20),
        name="qkv_forward",
    )(stream, vec, vec, vec, weights)


def offsets(rows):
    return lax.broadcasted_iota(jnp.int32, (rows, rows), 0) - lax.broadcasted_iota(
        jnp.int32, (rows, rows), 1
    )


def head_lanes(block, half):
    lanes = lax.broadcasted_iota(jnp.int32, block.shape, 1) // HEAD
    return jnp.where(lanes == half, block, jnp.zeros_like(block))


def attend_kernel(pb, far, *refs):
    thr_ref, q_ref, k_ref, v_ref = refs[:4]
    far_refs = refs[4 : 4 + far]
    out_ref, lse_ref = refs[4 + far :]
    steps = offsets(pb)
    keys = [k_ref[:pb, :]] + [ref[0] for ref in far_refs]
    values = [v_ref[:pb, :]] + [ref[1] for ref in far_refs]
    total = None
    for half in range(2):
        q = head_lanes(q_ref[...], half) * jnp.asarray(HEAD**-0.5, BF16)
        lefts, rights = [], []
        for j, k in enumerate(keys):
            s = dot_nt(k, q)
            lefts.append(jnp.where(steps <= thr_ref[j], s[:, :pb], NEGATIVE))
            rights.append(s[:, pb:])
        own = jnp.where(steps <= 0, dot_nt(k_ref[pb:, :], q[pb:, :]), NEGATIVE)
        top_p = jnp.max(functools.reduce(jnp.maximum, lefts), 0, keepdims=True)
        top_c = jnp.max(functools.reduce(jnp.maximum, rights + [own]), 0, keepdims=True)
        sum_p = jnp.zeros((1, pb), F32)
        own = jnp.exp(own - top_c)
        sum_c = jnp.sum(own, 0, keepdims=True)
        acc_p = jnp.zeros((PAIR, pb), F32)
        acc_c = dot_tn(head_lanes(v_ref[pb:, :], half), own.astype(BF16))
        for j, v in enumerate(values):
            v = head_lanes(v, half)
            left = jnp.exp(lefts[j] - top_p)
            right = jnp.exp(rights[j] - top_c)
            sum_p += jnp.sum(left, 0, keepdims=True)
            sum_c += jnp.sum(right, 0, keepdims=True)
            acc_p += dot_tn(v, left.astype(BF16))
            acc_c += dot_tn(v, right.astype(BF16))
        lse_ref[half, :, :] = jnp.concatenate(
            [top_p + jnp.log(sum_p), top_c + jnp.log(sum_c)], 1
        )
        part = jnp.concatenate([acc_p / sum_p, acc_c / sum_c], 1)
        total = part if total is None else total + part
    out_ref[...] = total.T.astype(BF16)


def attend_forward(thr, qkv, far, part, parts):
    rows, width = qkv.shape[0], qkv.shape[1] // 3
    pb = rows // 2
    pairs = width // PAIR // parts
    place = lambda kind: pl.BlockSpec((rows, PAIR), lambda i: (0, (kind * parts + part) * pairs + i))
    block = pl.BlockSpec((2, pb, PAIR), lambda i: (0, 0, i))
    return pl.pallas_call(
        functools.partial(attend_kernel, pb, len(far)),
        grid=(pairs,),
        in_specs=[pl.BlockSpec(memory_space=pltpu.SMEM), place(0), place(1), place(2)]
        + [block] * len(far),
        out_specs=[
            pl.BlockSpec((rows, PAIR), lambda i: (0, i)),
            pl.BlockSpec((2, 1, rows), lambda i: (i, 0, 0)),
        ],
        out_shape=[
            jax.ShapeDtypeStruct((rows, width // parts), BF16),
            jax.ShapeDtypeStruct((2 * pairs, 1, rows), F32),
        ],
        compiler_params=params(),
        cost_estimate=cost(
            48 * rows * (len(far) + 2) * pb * width // parts,
            10 * 2**20 // parts,
            rows * (len(far) + 1) * pb * 16 // parts,
        ),
        name="attend_forward",
    )(thr, qkv, qkv, qkv, *far)


def attend_pull_kernel(pb, far, *refs):
    thr_ref, q_ref, k_ref, v_ref = refs[:4]
    far_refs = refs[4 : 4 + far]
    lse_ref, do_ref, o_ref = refs[4 + far : 7 + far]
    dq_ref, dcont_ref = refs[7 + far : 9 + far]
    dfar_refs = refs[9 + far :]
    steps = offsets(pb)
    scale = HEAD**-0.5
    keys = [k_ref[:pb, :]] + [ref[0] for ref in far_refs]
    values = [v_ref[:pb, :]] + [ref[1] for ref in far_refs]
    both = (do_ref[...].astype(F32) * o_ref[...].astype(F32)).T
    dq = jnp.zeros((PAIR, 2 * pb), F32)
    dks = [jnp.zeros((pb, PAIR), F32) for _ in keys]
    dvs = [jnp.zeros((pb, PAIR), F32) for _ in keys]
    dkc = jnp.zeros((pb, PAIR), F32)
    dvc = jnp.zeros((pb, PAIR), F32)
    dqc = jnp.zeros((PAIR, pb), F32)
    for half in range(2):
        q = head_lanes(q_ref[...], half) * jnp.asarray(scale, BF16)
        do = head_lanes(do_ref[...], half)
        lse = lse_ref[half, :, :]
        delta = jnp.sum(both[half * HEAD : (half + 1) * HEAD, :], 0, keepdims=True)
        for j, (k, v) in enumerate(zip(keys, values)):
            s = dot_nt(k, q)
            left = jnp.where(steps <= thr_ref[j], s[:, :pb], NEGATIVE)
            p = jnp.exp(jnp.concatenate([left, s[:, pb:]], 1) - lse)
            dp = dot_nt(v, do)
            ds = (p * (dp - delta)).astype(BF16)
            dvs[j] += dot(p.astype(BF16), do)
            dks[j] += dot(ds, q)
            dq += dot_tn(head_lanes(k, half), ds)
        kc, vc = k_ref[pb:, :], v_ref[pb:, :]
        s = jnp.where(steps <= 0, dot_nt(kc, q[pb:, :]), NEGATIVE)
        p = jnp.exp(s - lse[:, pb:])
        dp = dot_nt(vc, do[pb:, :])
        ds = (p * (dp - delta[:, pb:])).astype(BF16)
        dvc += dot(p.astype(BF16), do[pb:, :])
        dkc += dot(ds, q[pb:, :])
        dqc += dot_tn(head_lanes(kc, half), ds)
    for ref, dk, dv in zip(dfar_refs, dks, dvs):
        ref[0] = dk.astype(BF16)
        ref[1] = dv.astype(BF16)
    dcont_ref[0] = dkc.astype(BF16)
    dcont_ref[1] = dvc.astype(BF16)
    dq = jnp.concatenate([dq[:, :pb], dq[:, pb:] + dqc], 1)
    dq_ref[...] = (dq.T * scale).astype(BF16)


def attend_backward(thr, qkv, far, lse, do, attended, part, parts):
    rows, width = qkv.shape[0], qkv.shape[1] // 3
    pb = rows // 2
    pairs = width // PAIR // parts
    place = lambda kind: pl.BlockSpec((rows, PAIR), lambda i: (0, (kind * parts + part) * pairs + i))
    block = pl.BlockSpec((2, pb, PAIR), lambda i: (0, 0, i))
    column = pl.BlockSpec((rows, PAIR), lambda i: (0, i))
    pieces = len(far) + 2
    return pl.pallas_call(
        functools.partial(attend_pull_kernel, pb, len(far)),
        grid=(pairs,),
        in_specs=[pl.BlockSpec(memory_space=pltpu.SMEM), place(0), place(1), place(2)]
        + [block] * len(far)
        + [pl.BlockSpec((2, 1, rows), lambda i: (i, 0, 0)), place(0), column],
        out_specs=[column] + [block] * pieces,
        out_shape=[jax.ShapeDtypeStruct((rows, width // parts), BF16)]
        + [jax.ShapeDtypeStruct((2, pb, width // parts), BF16)] * pieces,
        compiler_params=params(),
        cost_estimate=cost(
            80 * rows * pieces * pb * width // parts,
            18 * 2**20 // parts,
            rows * pieces * pb * 16 // parts,
        ),
        name="attend_backward",
    )(thr, qkv, qkv, qkv, *far, lse, do, attended)


SLABS = 4
EARLY = 3


def feed_kernel(parts, x_ref, *refs):
    att_refs = refs[:parts]
    (wm_ref, mb_ref, gain_ref, shift_ref, eb_ref, rb_ref, w_ref,
     out_ref, middle_ref, second_ref, hidden_ref) = refs[parts:]
    width = x_ref.shape[1]

    @pl.when(pl.program_id(0) == 0)
    def _():
        middle = x_ref[...] + mb_ref[...]
        size = att_refs[0].shape[1]
        for part, ref in enumerate(att_refs):
            middle += dot(ref[...], wm_ref[part * size : (part + 1) * size, :])
        middle_ref[...] = middle
        normal, _ = center(middle)
        second_ref[...] = (normal * gain_ref[...] + shift_ref[...]).astype(BF16)
        out_ref[...] = middle + rb_ref[...]

    cut = width // 2
    for start in range(0, width, cut):
        hidden = dot(second_ref[...], w_ref[:, start : start + cut]) + eb_ref[:, start : start + cut]
        hidden_ref[:, start : start + cut] = hidden.astype(BF16)
        active = 0.5 * hidden * (1.0 + jnp.tanh(CURVE * hidden * (1.0 + CUBIC * hidden * hidden)))
        out_ref[...] += dot(active.astype(BF16), w_ref[start : start + cut, width:])


def feed_forward(stream, attended, vec, weights):
    rows, width = stream.shape
    array, at, mix_at = weights
    return pl.pallas_call(
        functools.partial(feed_kernel, len(attended)),
        grid=(SLABS,),
        in_specs=[whole((rows, width))]
        + [whole(piece.shape) for piece in attended]
        + [
            pl.BlockSpec((width, width), lambda j: (0, mix_at // width)),
            vector(width, V_MB),
            vector(width, V_SG),
            vector(width, V_SS),
            pl.BlockSpec((1, width), lambda j: (0, V_EB + j)),
            vector(width, V_RB),
            pl.BlockSpec((width, 2 * width), lambda j: (0, at // (2 * width) + j)),
        ],
        out_specs=[
            whole((rows, width)),
            whole((rows, width)),
            whole((rows, width)),
            pl.BlockSpec((rows, width), lambda j: (0, j)),
        ],
        out_shape=[
            jax.ShapeDtypeStruct((rows, width), F32),
            jax.ShapeDtypeStruct((rows, width), F32),
            jax.ShapeDtypeStruct((rows, width), BF16),
            jax.ShapeDtypeStruct((rows, SLABS * width), BF16),
        ],
        compiler_params=params(),
        cost_estimate=cost(18 * rows * width * width, 30 * 2**20, rows * SLABS * width),
        name="feed_forward",
    )(stream, *attended, array, vec, vec, vec, vec, vec, array)


def put_rows(refs, grad, core):
    if len(refs) == 1:
        refs[0][...] = grad
        return
    mine, other = refs
    planes, span, block = mine.shape
    split = grad.reshape(planes, 2, span, block)
    first = core == 0
    mine[...] = jnp.where(first, split[:, 0], split[:, 1])
    other[...] = jnp.where(first, split[:, 1], split[:, 0])


def grad_outs(holders, width, columns, block, apart):
    if not apart:
        return [pl.BlockSpec((width, block), lambda j: (0, j))], [
            jax.ShapeDtypeStruct((width, columns), BF16)
        ]
    shape = (holders // 2, width // holders)
    spec = pl.BlockSpec(shape + (block,), lambda j: (0, 0, j))
    return [spec] * 2, [jax.ShapeDtypeStruct(shape + (columns,), BF16)] * 2


def feed_pull_kernel(final, slabs, parts, outs, core_ref, gs_ref, *refs):
    att_refs, refs = refs[:parts], refs[parts:]
    hidden_ref, second_ref, w_ref = refs[:3]
    refs = refs[3:]
    if final:
        middle_ref, gain_ref, wm_ref, before_ref = refs[:4]
        refs = refs[4:]
    dw_refs, deb_ref, refs = refs[:outs], refs[outs], refs[outs + 1 :]
    if final:
        gm_ref, gatt_ref, dsg_ref, dss_ref, dmb_ref, acc_ref = refs[:6]
    else:
        acc_ref, drb_ref = refs[:2]
    gb_scr, sec_scr, act_scr = refs[-3:]
    step = pl.program_id(0)
    core = core_ref[0]
    width = gs_ref.shape[1]

    @pl.when(step == 0)
    def _():
        branch = gs_ref[...].astype(BF16)
        gb_scr[...] = branch
        sec_scr[...] = second_ref[...].T
        if final:
            acc_ref[...] = before_ref[...]
        else:
            acc_ref[...] = jnp.zeros_like(acc_ref)
            drb_ref[...] = jnp.sum(branch.astype(F32), 0, keepdims=True)

    def hidden_part(columns):
        grad_active = dot_nt(gb_scr[...], w_ref[columns, width:])
        v = hidden_ref[:, columns].astype(F32)
        square = v * v
        t = jnp.tanh(CURVE * v * (1.0 + CUBIC * square))
        half = 0.5 + 0.5 * t
        slope = half + 0.5 * v * (1.0 - t * t) * (CURVE * (1.0 + 3 * CUBIC * square))
        grad_hidden = (grad_active * slope).astype(BF16)
        deb_ref[:, columns] = jnp.sum(grad_hidden.astype(F32), 0, keepdims=True)
        acc_ref[...] += dot_nt(grad_hidden, w_ref[:, columns])
        return (v * half).astype(BF16), grad_hidden

    cut = width // 2
    pieces = [slice(start, start + cut) for start in range(0, width, cut)]

    if not final:
        for columns in pieces:
            active, grad_hidden = hidden_part(columns)
            dw_refs[0][columns, width:] = dot_tn(active, gb_scr[...]).astype(BF16)
            dw_refs[0][:, columns] = dot(sec_scr[...], grad_hidden).astype(BF16)
        return

    @pl.when((step % 2 == 0) & (step < 2 * slabs))
    def _():
        for columns in pieces:
            act_scr[:, columns], grad_hidden = hidden_part(columns)
            put_rows(
                [ref.at[..., columns] for ref in dw_refs],
                dot(sec_scr[...], grad_hidden).astype(BF16),
                core,
            )

    @pl.when(step % 2 == 1)
    def _():
        put_rows(dw_refs, dot_tn(act_scr[...], gb_scr[...]).astype(BF16), core)


    @pl.when(step == 2 * slabs)
    def _():
        term, dgain, dshift = norm_pull(middle_ref[...], gain_ref[...], acc_ref[...])
        dsg_ref[...] = dgain
        dss_ref[...] = dshift
        grad_middle = gs_ref[...] + term
        gm_ref[...] = grad_middle
        grad_mix = grad_middle.astype(BF16)
        dmb_ref[...] = jnp.sum(grad_mix.astype(F32), 0, keepdims=True)
        gatt_ref[...] = dot_nt(grad_mix, wm_ref[...]).astype(BF16)
        size = att_refs[0].shape[1]
        for part, ref in enumerate(att_refs):
            sec_scr[part * size : (part + 1) * size, :] = ref[...].T
        put_rows(dw_refs, dot(sec_scr[...], grad_mix).astype(BF16), core)


def feed_backward(holders, core, grad_stream, hidden, second, vec, weights, apart, final=()):
    rows, width = grad_stream.shape
    array, at, mix_at = weights
    half = SLABS - EARLY if final else EARLY
    row = whole((1, width))
    small = jax.ShapeDtypeStruct((1, width), F32)
    base = EARLY if final else 0
    each = 2 if final else 1
    slab = lambda j: base + jnp.minimum(j // each, half - 1)
    blocks = 2 * half + 1 if final else 2 * half
    dw_specs, dw_shapes = grad_outs(holders, width, blocks * width, 2 * width // each, apart)
    square = whole((rows, width))
    in_specs = [
        pl.BlockSpec((rows, width), lambda j: (0, slab(j))),
        square,
        pl.BlockSpec((width, 2 * width), lambda j: (0, at // (2 * width) + slab(j))),
    ]
    operands = [hidden, second, array]
    out_specs = dw_specs + [pl.BlockSpec((1, width), lambda j: (0, slab(j) - base))]
    out_shape = dw_shapes + [jax.ShapeDtypeStruct((1, half * width), F32)]
    total = jax.ShapeDtypeStruct((rows, width), F32)
    scratch = [
        pltpu.VMEM((rows, width), BF16),
        pltpu.VMEM((width, rows), BF16),
        pltpu.VMEM((rows, width), BF16),
    ]
    attended = []
    if final:
        middle, attended, so_far = final
        in_specs += [
            square,
            vector(width, V_SG),
            pl.BlockSpec((width, width), lambda j: (0, mix_at // width)),
            square,
        ]
        operands += [middle, vec, array, so_far]
        out_specs += [square, square, row, row, row]
        out_shape += [total, jax.ShapeDtypeStruct((rows, width), BF16), small, small, small]
        scratch = [pltpu.VMEM((rows, width), F32)] + scratch
    else:
        out_specs += [square, row]
        out_shape += [total, small]
    return pl.pallas_call(
        functools.partial(feed_pull_kernel, bool(final), half, len(attended), len(dw_specs)),
        grid=(blocks if final else half,),
        in_specs=[pl.BlockSpec(memory_space=pltpu.SMEM), square]
        + [whole(piece.shape) for piece in attended]
        + in_specs,
        out_specs=out_specs,
        out_shape=out_shape,
        scratch_shapes=scratch,
        compiler_params=params(),
        cost_estimate=cost(blocks * 4 * rows * width * width, blocks * 5 * 2**20, rows * half * width),
        name="feed_backward",
    )(core, grad_stream, *attended, *operands)


def qkv_pull_kernel(parts, sums, outs, core_ref, *refs):
    dq_refs, refs = refs[:parts], refs[parts:]
    cont_refs, refs = refs[:parts], refs[parts:]
    sum_refs, refs = refs[: parts * sums], refs[parts * sums :]
    normed_ref, x_ref, gm_ref, gain_ref, w_ref = refs[:5]
    dw_refs = refs[5 : 5 + outs]
    out_ref, dbias_ref, dgain_ref, dshift_ref, norm_scr, acc_scr, g_scr = refs[5 + outs :]
    step = pl.program_id(0)

    @pl.when(step == 0)
    def _():
        norm_scr[...] = normed_ref[...].T
        acc_scr[...] = jnp.zeros_like(acc_scr)
        for part in range(parts):
            g_scr[part] = dq_refs[part][...]
            total = sum(ref[...].astype(F32) for ref in sum_refs[part * sums : (part + 1) * sums])
            for kind in range(2):
                both = jnp.concatenate([total[kind].astype(BF16), cont_refs[part][kind]], 0)
                g_scr[(1 + kind) * parts + part] = both

    grad = g_scr[step]
    dbias_ref[...] = jnp.sum(grad.astype(F32), 0, keepdims=True)
    put_rows(dw_refs, dot(norm_scr[...], grad).astype(BF16), core_ref[0])
    acc_scr[...] += dot_nt(grad, w_ref[...])

    @pl.when(step == pl.num_programs(0) - 1)
    def _():
        term, dgain, dshift = norm_pull(x_ref[...], gain_ref[...], acc_scr[...])
        dgain_ref[...] = dgain
        dshift_ref[...] = dshift
        out_ref[...] = gm_ref[...] + term


def qkv_backward(holders, core, dqs, conts, sums, normed, stream, grad_middle, vec, weights, apart):
    rows, width = stream.shape
    parts = len(dqs)
    block = width // parts
    wq, place = weights
    small = jax.ShapeDtypeStruct((1, width), F32)
    flat = [piece for part in sums for piece in part]
    dw_specs, dw_shapes = grad_outs(holders, width, 3 * width, block, apart)
    return pl.pallas_call(
        functools.partial(qkv_pull_kernel, parts, len(sums[0]), len(dw_specs)),
        grid=(3 * parts,),
        in_specs=[pl.BlockSpec(memory_space=pltpu.SMEM)]
        + [whole(piece.shape) for piece in dqs + conts + flat]
        + [
            whole((rows, width)),
            whole((rows, width)),
            whole((rows, width)),
            vector(width, V_FG),
            pl.BlockSpec((width, block), lambda j: (0, place // block + j)),
        ],
        out_specs=dw_specs
        + [
            whole((rows, width)),
            pl.BlockSpec((1, block), lambda j: (0, j)),
            whole((1, width)),
            whole((1, width)),
        ],
        out_shape=dw_shapes
        + [
            jax.ShapeDtypeStruct((rows, width), F32),
            jax.ShapeDtypeStruct((1, 3 * width), F32),
            small,
            small,
        ],
        scratch_shapes=[
            pltpu.VMEM((width, rows), BF16),
            pltpu.VMEM((rows, width), F32),
            pltpu.VMEM((3 * parts, rows, block), BF16),
        ],
        compiler_params=params(),
        cost_estimate=cost(12 * rows * width * width, 24 * 2**20),
        name="qkv_backward",
    )(core, *dqs, *conts, *flat, normed, stream, grad_middle, vec, wq)


def trade(block, axis, bits):
    return lax.ppermute(block, axis, [(i, i ^ bits) for i in range(lax.axis_size(axis))])


def pick(block, place, axis):
    return lax.dynamic_index_in_dim(block, place, axis, keepdims=False)


def added(*blocks):
    return sum(block.astype(F32) for block in blocks).astype(BF16)


def split_kernel(count, lows, bits_ref, *refs):
    for side, low in enumerate(lows):
        ins = refs[side * count : (side + 1) * count]
        keep_ref, send_ref = refs[2 * count + 2 * side : 2 * count + 2 * side + 2]
        bit = bits_ref[side]
        for k in range(keep_ref.shape[1]):
            base = (k >> low << (low + 1)) | (k & ((1 << low) - 1))
            for ref, value in ((keep_ref, bit), (send_ref, 1 - bit)):
                place = base + (value << low)
                ref[:, k] = sum(one[:, place].astype(F32) for one in ins).astype(BF16)


def split_sum(sides, bits, lows, starts, cut):
    planes, holders, share, _ = sides[0][0].shape
    piece = next(size for size in range(cut, 0, -128) if all(start % size == 0 for start in starts))
    deep = max(1, planes // 2)
    specs = [
        pl.BlockSpec((deep, holders, share, piece), lambda i, j, start=start: (i, 0, 0, start // piece + j))
        for blocks, start in zip(sides, starts)
        for _ in blocks
    ]
    out = pl.BlockSpec((deep, holders // 2, share, piece), lambda i, j: (i, 0, 0, j))
    return pl.pallas_call(
        functools.partial(split_kernel, len(sides[0]), lows),
        grid=(planes // deep, cut // piece),
        in_specs=[pl.BlockSpec(memory_space=pltpu.SMEM)] + specs,
        out_specs=[out] * 4,
        out_shape=[jax.ShapeDtypeStruct((planes, holders // 2, share, cut), BF16)] * 4,
        compiler_params=params(("arbitrary",) * 2),
        cost_estimate=cost(planes * holders * share * cut * 4, 12 * planes * holders * share * cut),
        name="split_sum",
    )(jnp.stack(bits), *sides[0], *sides[1])


def plane_kernel(plane_ref, *refs):
    ins, outs = refs[:4], refs[4:]
    cut = ins[0].shape[-1]
    for step, ref in enumerate(outs):
        place = jnp.bitwise_xor(plane_ref[0], step)
        for side in range(2):
            value = ins[2 * side][place, 0].astype(F32) + ins[2 * side + 1][place, 0].astype(F32)
            ref[:, side * cut : (side + 1) * cut] = value.astype(BF16)


def plane_rows(blocks, plane):
    planes, _, share, cut = blocks[0].shape
    return pl.pallas_call(
        plane_kernel,
        grid=(1,),
        in_specs=[pl.BlockSpec(memory_space=pltpu.SMEM)] + [whole(block.shape) for block in blocks],
        out_specs=[whole((share, 2 * cut))] * planes,
        out_shape=[jax.ShapeDtypeStruct((share, 2 * cut), BF16)] * planes,
        compiler_params=params(),
        cost_estimate=cost(planes * share * cut * 4, planes * share * cut * 12),
        name="plane_rows",
    )(plane.reshape(1), *blocks)


def reduce_stages(*pairs):
    planes, span, columns = pairs[0][0].shape
    n_tok = lax.axis_size("tok")
    me, plane = lax.axis_index("tok"), lax.axis_index("wa") // 2
    bits = n_tok.bit_length() - 1
    cut = columns * len(pairs) // 2
    sides = [
        [
            block.reshape(planes, n_tok, span // n_tok, columns)
            for block in (mine, trade(other, "wa", 1))
        ]
        for mine, other in pairs
    ]
    starts = [0, 0]
    if len(pairs) == 1:
        sides, starts = sides * 2, [0, cut]
    orders = [list(range(bits)), list(reversed(range(bits)))]
    left = [list(range(bits)), list(range(bits))]
    for turn in range(bits):
        lows = []
        for order, rest in zip(orders, left):
            lows.append(rest.index(order[turn]))
            rest.remove(order[turn])
        own = [(me >> order[turn]) & 1 for order in orders]
        keep0, send0, keep1, send1 = split_sum(sides, own, lows, starts, cut)
        starts = [0, 0]
        sends = yield [send0, send1]
        sides = [
            [keep, trade(send, "tok", 1 << order[turn])]
            for keep, send, order in zip((keep0, keep1), sends, orders)
        ]
    sends = plane_rows(sides[0] + sides[1], plane)
    sends = yield sends
    got = [trade(send, "wa", 2 * step) for step, send in enumerate(sends) if step]
    return added(sends[0], *got)


def assemble_kernel(planes, holders, places_ref, *refs):
    own_ref, sibling_ref = refs[:2]
    near_refs, far_refs = refs[2 : 2 + holders], refs[2 + holders : 2 + 2 * holders]
    out_ref, sems = refs[-2:]
    wa, me = places_ref[0], places_ref[1]
    copies = []

    def copy(source, target):
        copies.append(pltpu.make_async_copy(source, target, sems.at[len(copies)]))
        copies[-1].start()

    copy(own_ref, out_ref.at[wa])
    copy(sibling_ref, out_ref.at[jnp.bitwise_xor(wa, 1)])
    for core, group in enumerate((near_refs, far_refs)):
        for turn, ref in enumerate(group):
            for step in range(1, planes):
                place = out_ref.at[jnp.bitwise_xor(wa, 2 * step + core), jnp.bitwise_xor(me, turn)]
                copy(ref.at[step - 1], place)
    for one in copies:
        one.wait()


def assemble(own, sibling, near, far):
    holders, share, columns = own.shape
    planes = near[0].shape[0] + 1
    anywhere = pl.BlockSpec(memory_space=pl.ANY)
    places = jnp.stack([lax.axis_index("wa"), lax.axis_index("tok")])
    whole_array = pl.pallas_call(
        functools.partial(assemble_kernel, planes, holders),
        in_specs=[pl.BlockSpec(memory_space=pltpu.SMEM)] + [anywhere] * (2 + 2 * holders),
        out_specs=anywhere,
        out_shape=jax.ShapeDtypeStruct((2 * planes, holders, share, columns), BF16),
        scratch_shapes=[pltpu.SemaphoreType.DMA((2 + 2 * holders * (planes - 1),))],
        compiler_params=pltpu.CompilerParams(vmem_limit_bytes=2**22),
        cost_estimate=cost(0, 8 * planes * holders * share * columns),
        name="assemble",
    )(places, own, sibling, *near, *far)
    return whole_array.reshape(-1, columns)


class Gathering:
    def __init__(self, shard):
        n_tok = lax.axis_size("tok")
        self.own = shard.reshape(n_tok, -1, shard.shape[1])
        self.ready = pick(self.own, lax.axis_index("tok"), 0)
        self.stage = 0

    def go(self, ready):
        planes, n_tok = lax.axis_size("wa") // 2, lax.axis_size("tok")
        if self.stage == 0:
            self.sibling = trade(self.own, "wa", 1)
            self.ready = jnp.stack([trade(ready, "wa", 2 * step) for step in range(1, planes)])
        elif self.stage == 1:
            self.near = [ready] + [trade(ready, "tok", step) for step in range(1, n_tok)]
            self.far = [trade(ready, "wa", 1)]
            self.ready = self.near
        elif self.stage == 2:
            self.near = ready
            self.far += [trade(block, "wa", 1) for block in ready[1:]]
            self.ready = None
        self.stage += 1

    def finish(self):
        while self.ready is not None:
            self.go(self.ready)
        return assemble(self.own, self.sibling, self.near, self.far)


def pack_kernel(span, me_ref, expand_ref, reduce_ref, mix_ref, qkv_ref, *out_refs):
    del me_ref
    width = mix_ref.shape[2]
    wide = (2 * SLABS + 1) * width
    for layer, out_ref in enumerate(out_refs):
        for a in range(SLABS):
            start = 2 * a * width
            for w in range(width // span):
                place = (w * SLABS + a) * span
                piece = expand_ref[layer, :, place : place + span]
                out_ref[:, start + w * span : start + (w + 1) * span] = piece
            out_ref[:, start + width : start + 2 * width] = reduce_ref[layer, a, 0]
        out_ref[:, wide - width : wide] = mix_ref[layer]
        if not layer:
            out_ref[:, wide:] = qkv_ref[1]


def pack(expand, reduce, mix, qkv):
    n_tok, me = lax.axis_size("tok"), lax.axis_index("tok")
    layers, span, width = mix.shape
    share = span // n_tok
    wide = (2 * SLABS + 1) * width
    by_row = lambda size: pl.BlockSpec((layers, share, size), lambda i, me: (0, me[0], 0))
    shapes = [(share, wide + 3 * width), (share, wide)]
    return pl.pallas_call(
        functools.partial(pack_kernel, span),
        grid_spec=pltpu.PrefetchScalarGridSpec(
            num_scalar_prefetch=1,
            grid=(1,),
            in_specs=[
                by_row(SLABS * width),
                pl.BlockSpec((layers, SLABS, 1, share, width), lambda i, me: (0, 0, me[0], 0, 0)),
                by_row(width),
                by_row(3 * width),
            ],
            out_specs=[pl.BlockSpec(shape, lambda i, me: (0, 0)) for shape in shapes],
        ),
        out_shape=[jax.ShapeDtypeStruct(shape, BF16) for shape in shapes],
        compiler_params=params(),
        cost_estimate=cost(0, 8 * share * wide),
        name="pack",
    )(
        me.reshape(1), expand, reduce.reshape(layers, SLABS, n_tok, share, width), mix, qkv
    )


class Reduction:
    def __init__(self, *pairs):
        self.walk = reduce_stages(*pairs)
        self.result = None
        self.ready = next(self.walk)

    def go(self, values):
        try:
            self.ready = self.walk.send(values)
        except StopIteration as stop:
            self.ready = None
            self.result = stop.value

    def finish(self):
        while self.ready is not None:
            self.go(self.ready)
        return self.result


def together(value, reductions):
    active = [item for item in reductions if item.ready is not None]
    value, ready = lax.optimization_barrier((value, [item.ready for item in active]))
    for item, values in zip(active, ready):
        item.go(values)
    return value


def feed_out_kernel(pieces, me_ref, *refs):
    mix_ref, expand_ref, reduce_ref = refs[-3:]
    span, width = mix_ref.shape[1] * mix_ref.shape[2], mix_ref.shape[3]
    for step, ref in enumerate(refs[:pieces]):
        place = jnp.bitwise_xor(me_ref[0], step)
        for a in range(SLABS):
            for w in range(width // span):
                there = 2 * a * width + w * span
                value = ref[:, there : there + span].astype(F32)
                expand_ref[0, place, :, (w * SLABS + a) * span : (w * SLABS + a + 1) * span] = value
            there = (2 * a + 1) * width
            reduce_ref[0, a, place] = ref[:, there : there + width].astype(F32)
        mix_ref[0, place] = ref[:, 2 * SLABS * width :].astype(F32)


def feed_out(pieces, width, me, layer, held):
    n_tok = len(pieces)
    share = pieces[0].shape[0]
    shapes = [(n_tok, share, width), (n_tok, share, SLABS * width), (SLABS, n_tok, share, width)]
    return pl.pallas_call(
        functools.partial(feed_out_kernel, n_tok),
        grid=(1,),
        in_specs=[pl.BlockSpec(memory_space=pltpu.SMEM)]
        + [whole((share, (2 * SLABS + 1) * width)) for _ in pieces]
        + [pl.BlockSpec(memory_space=pl.ANY) for _ in held],
        out_specs=[
            pl.BlockSpec((1,) + shape, lambda i, rank=len(shape): (layer,) + (0,) * rank)
            for shape in shapes
        ],
        out_shape=[jax.ShapeDtypeStruct((LAYERS,) + shape, F32) for shape in shapes],
        input_output_aliases={1 + n_tok + k: k for k in range(len(held))},
        compiler_params=params(),
        cost_estimate=cost(9 * share * n_tok * width, 6 * 9 * share * n_tok * width),
        name="feed_out",
    )(me.reshape(1), *pieces, *held)


def qkv_out_kernel(pieces, me_ref, *refs):
    out_ref = refs[-1]
    for step, ref in enumerate(refs[:pieces]):
        out_ref[0, jnp.bitwise_xor(me_ref[0], step)] = ref[...].astype(F32)


def qkv_out(pieces, columns, me, layer, held):
    share = pieces[0].shape[0]
    shape = (len(pieces), share, columns)
    last = pieces[0].shape[1] // columns - 1
    return pl.pallas_call(
        functools.partial(qkv_out_kernel, len(pieces)),
        grid=(1,),
        in_specs=[pl.BlockSpec(memory_space=pltpu.SMEM)]
        + [pl.BlockSpec((share, columns), lambda i: (0, last)) for _ in pieces]
        + [pl.BlockSpec(memory_space=pl.ANY) for _ in held],
        out_specs=pl.BlockSpec((1,) + shape, lambda i: (layer, 0, 0, 0)),
        out_shape=jax.ShapeDtypeStruct((LAYERS,) + shape, F32),
        input_output_aliases={1 + len(pieces) + k: k for k in range(len(held))},
        compiler_params=params(),
        cost_estimate=cost(share * columns, 24 * share * columns),
        name="qkv_out",
    )(me.reshape(1), *pieces, *held)


def local(
    prompt_in, cont_in, first_gain, first_shift, qkv_weight, qv_bias, mix_weight, mix_bias,
    second_gain, second_shift, expand_weight, expand_bias, reduce_weight, reduce_bias, owners,
    prompt_cot, cont_cot,
):
    n_tok, n_wa = lax.axis_size("tok"), lax.axis_size("wa")
    me = lax.axis_index("tok")
    core = (lax.axis_index("wa") % 2).reshape(1)
    rows = prompt_in.shape[1]
    width = prompt_in.shape[2]
    span = width // n_wa
    parts = 2
    steps = list(range(1, n_tok))
    order = owners[0]
    by_step = jnp.stack([pick(order, me ^ step, 0) for step in [0] + steps])
    thr = (by_step[0] - by_step) * rows

    small = jnp.concatenate(
        [first_gain, first_shift, qv_bias, mix_bias, second_gain, second_shift, reduce_bias, expand_bias], 1
    )
    small = lax.all_gather(small, "wa", axis=0, tiled=False)

    def spread(layer):
        def piece(start, count):
            return small[:, layer, start * span : (start + count) * span].reshape(1, -1)

        pair = piece(2, 2)
        units = small[:, layer, 8 * span : 12 * span].reshape(n_wa, SLABS, span)
        pieces = [
            piece(0, 1), piece(1, 1), pair[:, :width], jnp.zeros((1, width), BF16), pair[:, width:],
            piece(4, 1), piece(5, 1), piece(6, 1), piece(7, 1),
            units.transpose(1, 0, 2).reshape(1, SLABS * width),
        ]
        return jnp.concatenate(pieces, 1).astype(F32)

    vecs = [spread(layer) for layer in range(LAYERS)]
    both = ("wa", "tok")
    share = span // n_tok

    wide = (2 * SLABS + 1) * width
    first = Gathering(qkv_weight[0])
    rows_middle, rows_last = pack(expand_weight, reduce_weight, mix_weight, qkv_weight)
    middle_array = lax.all_gather(rows_middle, both, axis=0, tiled=True)
    last_array = lax.all_gather(rows_last, both, axis=0, tiled=True)
    first = first.finish()

    stream = jnp.concatenate([prompt_in[0], cont_in[0, 0]], 0).astype(F32)
    kept = []
    size = width // parts
    weights = [
        ((first, 0), (middle_array, 0, wide - width)),
        ((middle_array, wide), (last_array, 0, wide - width)),
    ]
    for layer in range(LAYERS):
        wq, wf = weights[layer]
        qkv, normed = qkv_forward(stream, vecs[layer], *wq)
        fars, attended, lses = [], [], []
        for part in range(parts):
            block = jnp.stack(
                [
                    qkv[:rows, kind * width + part * size : kind * width + (part + 1) * size]
                    for kind in (1, 2)
                ]
            )
            fars.append([trade(block, "tok", step) for step in steps])
        for part in range(parts):
            one, lse = attend_forward(thr, qkv, fars[part], part, parts)
            attended.append(one)
            lses.append(lse)
        result, middle, second, hidden = feed_forward(stream, attended, vecs[layer], wf)
        kept.append((stream, normed, qkv, fars, lses, attended, middle, second, hidden))
        stream = result

    grad_stream = jnp.concatenate([prompt_cot[0], cont_cot[0, 0]], 0).astype(F32)
    smalls = [None] * LAYERS
    sync = lax.optimization_barrier

    def spread_rows(block):
        block = block.reshape(n_tok, share, block.shape[1])
        return [pick(block, me ^ step, 0) for step in [0] + steps]

    def from_each(blocks):
        return [blocks[0]] + [trade(block, "tok", step) for step, block in zip(steps, blocks[1:])]

    def to_each(block):
        return from_each([block] * n_tok)

    late, last, early = [None] * LAYERS, [None] * LAYERS, [None] * LAYERS
    for layer in reversed(range(LAYERS)):
        wq, wf = weights[layer]
        start, normed, qkv, fars, lses, attended, middle, second, hidden = kept[layer]
        if not layer:
            grad_stream = together(grad_stream, [late[1]])
        common = (n_wa, core, grad_stream, hidden, second, vecs[layer], wf)
        dw_early, deb_low, so_far, drb = feed_backward(*common, False)
        early[layer] = lax.psum_scatter(dw_early, "wa", scatter_dimension=0, tiled=True)
        if not layer:
            so_far, spread = together((so_far, spread_rows(early[1])), [late[1], last[1]])
            early[1] = added(*from_each(spread))
        late_mine, late_other, deb_high, grad_middle, grad_att, dsg, dss, dmb = feed_backward(
            *common, True, (middle, attended, so_far)
        )
        dqs, conts, sums = [], [], []
        for part in range(parts):
            if not layer:
                grad_att = together(grad_att, [last[1]])
            if layer or part:
                late[layer] = late[layer] or Reduction((late_mine, late_other))
            dq, cont, own, *far = attend_backward(
                thr, qkv, fars[part], lses[part], grad_att, attended[part], part, parts
            )
            dqs.append(dq)
            conts.append(cont)
            sums.append([own] + [trade(block, "tok", step) for step, block in zip(steps, far)])
        conts[-1] = together(conts[-1], [late[layer]])
        if not layer:
            upper = jnp.concatenate([early[1], late[1].finish(), last[1].finish()], 1)
            conts[-1], upper, rows_early = sync((conts[-1], upper, spread_rows(early[0])))
            early[0] = added(*from_each(rows_early))
            upper = to_each(upper)
        *dwq, grad_stream, dqb, dfg, dfs = qkv_backward(
            n_wa, core, dqs, conts, sums, normed, start, grad_middle, vecs[layer], wq, bool(layer)
        )
        if layer:
            last[layer] = Reduction(dwq)
        else:
            last[layer] = lax.psum_scatter(dwq[0], "wa", scatter_dimension=0, tiled=True)
        dqb = jnp.concatenate([dqb[:, :width], dqb[:, 2 * width :]], 1)
        deb = jnp.concatenate([deb_low, deb_high], 1)
        deb = deb.reshape(SLABS, n_wa, span).transpose(1, 0, 2)
        smalls[layer] = [
            piece.reshape(n_wa, -1) for piece in (dfg, dfs, dqb, dmb, dsg, dss, deb, drb)
        ]

    small = jnp.stack([jnp.concatenate(pieces, 1) for pieces in smalls], 1)
    bits = n_wa.bit_length() - 1
    small = small.reshape((2,) * bits + small.shape[1:])
    for bit in reversed(range(bits)):
        place = (lax.axis_index("wa") >> bit) & 1
        small = pick(small, place, 0) + trade(pick(small, 1 - place, 0), "wa", 1 << bit)
    for step in [1 << bit for bit in range(n_tok.bit_length() - 1)]:
        small = small + trade(small, "tok", step)

    lower = jnp.concatenate([early[0], late[0].finish()], 1)
    lower, last[0] = sync((lower, spread_rows(last[0])))
    last[0] = added(*from_each(last[0]))
    lower = to_each(lower)
    feeds = feed_out(upper, width, me, 1, [])
    qkvs = qkv_out(upper, 3 * width, me, 1, [])
    feeds = feed_out(lower, width, me, 0, feeds)
    qkvs = qkv_out(to_each(last[0]), 3 * width, me, 0, [qkvs])
    mixes, expands, reduces = [
        block.reshape(LAYERS, -1, width) if place != 1 else block.reshape(LAYERS, span, -1)
        for place, block in enumerate(feeds)
    ]
    qkvs = qkvs.reshape(LAYERS, span, 3 * width)

    def vec_out(start, count):
        return small[:, start * span : (start + count) * span]

    return (
        stream[:rows][None],
        stream[rows:][None, None],
        grad_stream[:rows][None],
        grad_stream[rows:][None, None],
        vec_out(0, 1),
        vec_out(1, 1),
        qkvs,
        vec_out(2, 2),
        mixes,
        vec_out(4, 1),
        vec_out(5, 1),
        vec_out(6, 1),
        expands,
        vec_out(7, 4),
        reduces,
        vec_out(11, 1),
    )


def solution(mesh):
    in_specs = (
        P("wa", "tok", None),
        P("wa", "tok", None, None),
        P(None, "wa"),
        P(None, "wa"),
        P(None, "wa", None),
        P(None, "wa"),
        P(None, "wa", None),
        P(None, "wa"),
        P(None, "wa"),
        P(None, "wa"),
        P(None, "wa", None),
        P(None, "wa"),
        P(None, "wa", None),
        P(None, "wa"),
        P("wa", None),
        P("wa", "tok", None),
        P("wa", "tok", None, None),
    )
    out_specs = (
        P("wa", "tok", None),
        P("wa", "tok", None, None),
        P("wa", "tok", None),
        P("wa", "tok", None, None),
        P(None, "wa"),
        P(None, "wa"),
        P(None, "wa", None),
        P(None, "wa"),
        P(None, "wa", None),
        P(None, "wa"),
        P(None, "wa"),
        P(None, "wa"),
        P(None, "wa", None),
        P(None, "wa"),
        P(None, "wa", None),
        P(None, "wa"),
    )
    return jax.shard_map(local, mesh=mesh, in_specs=in_specs, out_specs=out_specs, check_vma=False)
```

```python
import functools

import jax
import jax.numpy as jnp
from jax import lax
from jax.experimental import pallas as pl
from jax.experimental.pallas import tpu as pltpu
from jax.sharding import PartitionSpec as P

HEAD = 64
PAIR = 2 * HEAD
LAYERS = 2
EPSILON = 1e-05
NEGATIVE = -1e30
CURVE = 0.7978845608028654
CUBIC = 0.044715
F32 = jnp.float32
BF16 = jnp.bfloat16

V_FG, V_FS, V_QKV, V_MB, V_SG, V_SS, V_RB, V_EB = 0, 1, 2, 5, 6, 7, 8, 9


def dot(left, right):
    return jnp.dot(left, right, preferred_element_type=F32)


def dot_nt(left, right):
    return lax.dot_general(left, right, (((1,), (1,)), ((), ())), preferred_element_type=F32)


def dot_tn(left, right):
    return lax.dot_general(left, right, (((0,), (0,)), ((), ())), preferred_element_type=F32)


def params(semantics=("arbitrary",), mib=56):
    return pltpu.CompilerParams(dimension_semantics=semantics, vmem_limit_bytes=mib * 2**20)


def cost(flops, nbytes, trans=0):
    return pl.CostEstimate(flops=int(flops), bytes_accessed=int(nbytes), transcendentals=int(trans))


def center(rows):
    centred = rows - jnp.mean(rows, -1, keepdims=True)
    inverse = lax.rsqrt(jnp.mean(centred * centred, -1, keepdims=True) + EPSILON)
    return centred * inverse, inverse


def norm_pull(rows, gain, grad):
    normal, inverse = center(rows)
    inner = grad * gain
    term = inverse * (
        inner
        - jnp.mean(inner, -1, keepdims=True)
        - normal * jnp.mean(inner * normal, -1, keepdims=True)
    )
    return term, jnp.sum(grad * normal, 0, keepdims=True), jnp.sum(grad, 0, keepdims=True)


def whole(shape):
    return pl.BlockSpec(shape, lambda *_: (0,) * len(shape))


def vector(width, place):
    return pl.BlockSpec((1, width), lambda *_: (0, place))


def qkv_kernel(x_ref, gain_ref, shift_ref, bias_ref, w_ref, out_ref, normed_ref):
    @pl.when(pl.program_id(0) == 0)
    def _():
        normal, _ = center(x_ref[...])
        normed_ref[...] = (normal * gain_ref[...] + shift_ref[...]).astype(BF16)

    out_ref[...] = (dot(normed_ref[...], w_ref[...]) + bias_ref[...]).astype(BF16)


def qkv_forward(stream, vec, weights, place):
    rows, width = stream.shape
    block = 512
    steps = 3 * width // block
    return pl.pallas_call(
        qkv_kernel,
        grid=(steps,),
        in_specs=[
            whole((rows, width)),
            vector(width, V_FG),
            vector(width, V_FS),
            pl.BlockSpec((1, block), lambda j: (0, V_QKV * width // block + j)),
            pl.BlockSpec((width, block), lambda j: (0, place // block + j)),
        ],
        out_specs=[pl.BlockSpec((rows, block), lambda j: (0, j)), whole((rows, width))],
        out_shape=[
            jax.ShapeDtypeStruct((rows, 3 * width), BF16),
            jax.ShapeDtypeStruct((rows, width), BF16),
        ],
        compiler_params=params(),
        cost_estimate=cost(6 * rows * width * width, 16 * 2**20),
        name="qkv_forward",
    )(stream, vec, vec, vec, weights)


def offsets(rows):
    return lax.broadcasted_iota(jnp.int32, (rows, rows), 0) - lax.broadcasted_iota(
        jnp.int32, (rows, rows), 1
    )


def head_lanes(block, half):
    lanes = lax.broadcasted_iota(jnp.int32, block.shape, 1) // HEAD
    return jnp.where(lanes == half, block, jnp.zeros_like(block))


def attend_kernel(pb, far, *refs):
    thr_ref, q_ref, k_ref, v_ref = refs[:4]
    far_refs = refs[4 : 4 + far]
    out_ref, lse_ref = refs[4 + far :]
    steps = offsets(pb)
    keys = [k_ref[:pb, :]] + [ref[0] for ref in far_refs]
    values = [v_ref[:pb, :]] + [ref[1] for ref in far_refs]
    total = None
    for half in range(2):
        q = head_lanes(q_ref[...], half) * jnp.asarray(HEAD**-0.5, BF16)
        lefts, rights = [], []
        for j, k in enumerate(keys):
            s = dot_nt(k, q)
            lefts.append(jnp.where(steps <= thr_ref[j], s[:, :pb], NEGATIVE))
            rights.append(s[:, pb:])
        own = jnp.where(steps <= 0, dot_nt(k_ref[pb:, :], q[pb:, :]), NEGATIVE)
        top_p = jnp.max(functools.reduce(jnp.maximum, lefts), 0, keepdims=True)
        top_c = jnp.max(functools.reduce(jnp.maximum, rights + [own]), 0, keepdims=True)
        sum_p = jnp.zeros((1, pb), F32)
        own = jnp.exp(own - top_c)
        sum_c = jnp.sum(own, 0, keepdims=True)
        acc_p = jnp.zeros((PAIR, pb), F32)
        acc_c = dot_tn(head_lanes(v_ref[pb:, :], half), own.astype(BF16))
        for j, v in enumerate(values):
            v = head_lanes(v, half)
            left = jnp.exp(lefts[j] - top_p)
            right = jnp.exp(rights[j] - top_c)
            sum_p += jnp.sum(left, 0, keepdims=True)
            sum_c += jnp.sum(right, 0, keepdims=True)
            acc_p += dot_tn(v, left.astype(BF16))
            acc_c += dot_tn(v, right.astype(BF16))
        lse_ref[half, :, :] = jnp.concatenate(
            [top_p + jnp.log(sum_p), top_c + jnp.log(sum_c)], 1
        )
        part = jnp.concatenate([acc_p / sum_p, acc_c / sum_c], 1)
        total = part if total is None else total + part
    out_ref[...] = total.T.astype(BF16)


def attend_forward(thr, qkv, far, part, parts):
    rows, width = qkv.shape[0], qkv.shape[1] // 3
    pb = rows // 2
    pairs = width // PAIR // parts
    place = lambda kind: pl.BlockSpec((rows, PAIR), lambda i: (0, (kind * parts + part) * pairs + i))
    block = pl.BlockSpec((2, pb, PAIR), lambda i: (0, 0, i))
    return pl.pallas_call(
        functools.partial(attend_kernel, pb, len(far)),
        grid=(pairs,),
        in_specs=[pl.BlockSpec(memory_space=pltpu.SMEM), place(0), place(1), place(2)]
        + [block] * len(far),
        out_specs=[
            pl.BlockSpec((rows, PAIR), lambda i: (0, i)),
            pl.BlockSpec((2, 1, rows), lambda i: (i, 0, 0)),
        ],
        out_shape=[
            jax.ShapeDtypeStruct((rows, width // parts), BF16),
            jax.ShapeDtypeStruct((2 * pairs, 1, rows), F32),
        ],
        compiler_params=params(),
        cost_estimate=cost(
            48 * rows * (len(far) + 2) * pb * width // parts,
            10 * 2**20 // parts,
            rows * (len(far) + 1) * pb * 16 // parts,
        ),
        name="attend_forward",
    )(thr, qkv, qkv, qkv, *far)


def attend_pull_kernel(pb, far, *refs):
    thr_ref, q_ref, k_ref, v_ref = refs[:4]
    far_refs = refs[4 : 4 + far]
    lse_ref, do_ref, o_ref = refs[4 + far : 7 + far]
    dq_ref, dcont_ref = refs[7 + far : 9 + far]
    dfar_refs = refs[9 + far :]
    steps = offsets(pb)
    scale = HEAD**-0.5
    keys = [k_ref[:pb, :]] + [ref[0] for ref in far_refs]
    values = [v_ref[:pb, :]] + [ref[1] for ref in far_refs]
    both = (do_ref[...].astype(F32) * o_ref[...].astype(F32)).T
    dq = jnp.zeros((PAIR, 2 * pb), F32)
    dks = [jnp.zeros((pb, PAIR), F32) for _ in keys]
    dvs = [jnp.zeros((pb, PAIR), F32) for _ in keys]
    dkc = jnp.zeros((pb, PAIR), F32)
    dvc = jnp.zeros((pb, PAIR), F32)
    dqc = jnp.zeros((PAIR, pb), F32)
    for half in range(2):
        q = head_lanes(q_ref[...], half) * jnp.asarray(scale, BF16)
        do = head_lanes(do_ref[...], half)
        lse = lse_ref[half, :, :]
        delta = jnp.sum(both[half * HEAD : (half + 1) * HEAD, :], 0, keepdims=True)
        for j, (k, v) in enumerate(zip(keys, values)):
            s = dot_nt(k, q)
            left = jnp.where(steps <= thr_ref[j], s[:, :pb], NEGATIVE)
            p = jnp.exp(jnp.concatenate([left, s[:, pb:]], 1) - lse)
            dp = dot_nt(v, do)
            ds = (p * (dp - delta)).astype(BF16)
            dvs[j] += dot(p.astype(BF16), do)
            dks[j] += dot(ds, q)
            dq += dot_tn(head_lanes(k, half), ds)
        kc, vc = k_ref[pb:, :], v_ref[pb:, :]
        s = jnp.where(steps <= 0, dot_nt(kc, q[pb:, :]), NEGATIVE)
        p = jnp.exp(s - lse[:, pb:])
        dp = dot_nt(vc, do[pb:, :])
        ds = (p * (dp - delta[:, pb:])).astype(BF16)
        dvc += dot(p.astype(BF16), do[pb:, :])
        dkc += dot(ds, q[pb:, :])
        dqc += dot_tn(head_lanes(kc, half), ds)
    for ref, dk, dv in zip(dfar_refs, dks, dvs):
        ref[0] = dk.astype(BF16)
        ref[1] = dv.astype(BF16)
    dcont_ref[0] = dkc.astype(BF16)
    dcont_ref[1] = dvc.astype(BF16)
    dq = jnp.concatenate([dq[:, :pb], dq[:, pb:] + dqc], 1)
    dq_ref[...] = (dq.T * scale).astype(BF16)


def attend_backward(thr, qkv, far, lse, do, attended, part, parts):
    rows, width = qkv.shape[0], qkv.shape[1] // 3
    pb = rows // 2
    pairs = width // PAIR // parts
    place = lambda kind: pl.BlockSpec((rows, PAIR), lambda i: (0, (kind * parts + part) * pairs + i))
    block = pl.BlockSpec((2, pb, PAIR), lambda i: (0, 0, i))
    column = pl.BlockSpec((rows, PAIR), lambda i: (0, i))
    pieces = len(far) + 2
    return pl.pallas_call(
        functools.partial(attend_pull_kernel, pb, len(far)),
        grid=(pairs,),
        in_specs=[pl.BlockSpec(memory_space=pltpu.SMEM), place(0), place(1), place(2)]
        + [block] * len(far)
        + [pl.BlockSpec((2, 1, rows), lambda i: (i, 0, 0)), place(0), column],
        out_specs=[column] + [block] * pieces,
        out_shape=[jax.ShapeDtypeStruct((rows, width // parts), BF16)]
        + [jax.ShapeDtypeStruct((2, pb, width // parts), BF16)] * pieces,
        compiler_params=params(),
        cost_estimate=cost(
            80 * rows * pieces * pb * width // parts,
            18 * 2**20 // parts,
            rows * pieces * pb * 16 // parts,
        ),
        name="attend_backward",
    )(thr, qkv, qkv, qkv, *far, lse, do, attended)


SLABS = 4
EARLY = 3


def feed_kernel(parts, x_ref, *refs):
    att_refs = refs[:parts]
    (wm_ref, mb_ref, gain_ref, shift_ref, eb_ref, rb_ref, w_ref,
     out_ref, middle_ref, second_ref, hidden_ref) = refs[parts:]
    width = x_ref.shape[1]

    @pl.when(pl.program_id(0) == 0)
    def _():
        middle = x_ref[...] + mb_ref[...]
        size = att_refs[0].shape[1]
        for part, ref in enumerate(att_refs):
            middle += dot(ref[...], wm_ref[part * size : (part + 1) * size, :])
        middle_ref[...] = middle
        normal, _ = center(middle)
        second_ref[...] = (normal * gain_ref[...] + shift_ref[...]).astype(BF16)
        out_ref[...] = middle + rb_ref[...]

    cut = width // 2
    for start in range(0, width, cut):
        hidden = dot(second_ref[...], w_ref[:, start : start + cut]) + eb_ref[:, start : start + cut]
        hidden_ref[:, start : start + cut] = hidden.astype(BF16)
        active = 0.5 * hidden * (1.0 + jnp.tanh(CURVE * hidden * (1.0 + CUBIC * hidden * hidden)))
        out_ref[...] += dot(active.astype(BF16), w_ref[start : start + cut, width:])


def feed_forward(stream, attended, vec, weights):
    rows, width = stream.shape
    array, at, mix_at = weights
    return pl.pallas_call(
        functools.partial(feed_kernel, len(attended)),
        grid=(SLABS,),
        in_specs=[whole((rows, width))]
        + [whole(piece.shape) for piece in attended]
        + [
            pl.BlockSpec((width, width), lambda j: (0, mix_at // width)),
            vector(width, V_MB),
            vector(width, V_SG),
            vector(width, V_SS),
            pl.BlockSpec((1, width), lambda j: (0, V_EB + j)),
            vector(width, V_RB),
            pl.BlockSpec((width, 2 * width), lambda j: (0, at // (2 * width) + j)),
        ],
        out_specs=[
            whole((rows, width)),
            whole((rows, width)),
            whole((rows, width)),
            pl.BlockSpec((rows, width), lambda j: (0, j)),
        ],
        out_shape=[
            jax.ShapeDtypeStruct((rows, width), F32),
            jax.ShapeDtypeStruct((rows, width), F32),
            jax.ShapeDtypeStruct((rows, width), BF16),
            jax.ShapeDtypeStruct((rows, SLABS * width), BF16),
        ],
        compiler_params=params(),
        cost_estimate=cost(18 * rows * width * width, 30 * 2**20, rows * SLABS * width),
        name="feed_forward",
    )(stream, *attended, array, vec, vec, vec, vec, vec, array)


def put_rows(refs, grad, core):
    if len(refs) == 1:
        refs[0][...] = grad
        return
    mine, other = refs
    planes, span, block = mine.shape
    split = grad.reshape(planes, 2, span, block)
    first = core == 0
    mine[...] = jnp.where(first, split[:, 0], split[:, 1])
    other[...] = jnp.where(first, split[:, 1], split[:, 0])


def grad_outs(holders, width, columns, block, apart):
    if not apart:
        return [pl.BlockSpec((width, block), lambda j: (0, j))], [
            jax.ShapeDtypeStruct((width, columns), BF16)
        ]
    shape = (holders // 2, width // holders)
    spec = pl.BlockSpec(shape + (block,), lambda j: (0, 0, j))
    return [spec] * 2, [jax.ShapeDtypeStruct(shape + (columns,), BF16)] * 2


def feed_pull_kernel(final, slabs, parts, outs, core_ref, gs_ref, *refs):
    att_refs, refs = refs[:parts], refs[parts:]
    hidden_ref, second_ref, w_ref = refs[:3]
    refs = refs[3:]
    if final:
        middle_ref, gain_ref, wm_ref, before_ref = refs[:4]
        refs = refs[4:]
    dw_refs, deb_ref, refs = refs[:outs], refs[outs], refs[outs + 1 :]
    if final:
        gm_ref, gatt_ref, dsg_ref, dss_ref, dmb_ref, acc_ref = refs[:6]
    else:
        acc_ref, drb_ref = refs[:2]
    gb_scr, sec_scr, act_scr = refs[-3:]
    step = pl.program_id(0)
    core = core_ref[0]
    width = gs_ref.shape[1]

    @pl.when(step == 0)
    def _():
        branch = gs_ref[...].astype(BF16)
        gb_scr[...] = branch
        sec_scr[...] = second_ref[...].T
        if final:
            acc_ref[...] = before_ref[...]
        else:
            acc_ref[...] = jnp.zeros_like(acc_ref)
            drb_ref[...] = jnp.sum(branch.astype(F32), 0, keepdims=True)

    def hidden_part(columns):
        grad_active = dot_nt(gb_scr[...], w_ref[columns, width:])
        v = hidden_ref[:, columns].astype(F32)
        square = v * v
        t = jnp.tanh(CURVE * v * (1.0 + CUBIC * square))
        half = 0.5 + 0.5 * t
        slope = half + 0.5 * v * (1.0 - t * t) * (CURVE * (1.0 + 3 * CUBIC * square))
        grad_hidden = (grad_active * slope).astype(BF16)
        deb_ref[:, columns] = jnp.sum(grad_hidden.astype(F32), 0, keepdims=True)
        acc_ref[...] += dot_nt(grad_hidden, w_ref[:, columns])
        return (v * half).astype(BF16), grad_hidden

    cut = width // 2
    pieces = [slice(start, start + cut) for start in range(0, width, cut)]

    if not final:
        for columns in pieces:
            active, grad_hidden = hidden_part(columns)
            dw_refs[0][columns, width:] = dot_tn(active, gb_scr[...]).astype(BF16)
            dw_refs[0][:, columns] = dot(sec_scr[...], grad_hidden).astype(BF16)
        return

    @pl.when((step % 2 == 0) & (step < 2 * slabs))
    def _():
        for columns in pieces:
            act_scr[:, columns], grad_hidden = hidden_part(columns)
            put_rows(
                [ref.at[..., columns] for ref in dw_refs],
                dot(sec_scr[...], grad_hidden).astype(BF16),
                core,
            )

    @pl.when(step % 2 == 1)
    def _():
        put_rows(dw_refs, dot_tn(act_scr[...], gb_scr[...]).astype(BF16), core)


    @pl.when(step == 2 * slabs)
    def _():
        term, dgain, dshift = norm_pull(middle_ref[...], gain_ref[...], acc_ref[...])
        dsg_ref[...] = dgain
        dss_ref[...] = dshift
        grad_middle = gs_ref[...] + term
        gm_ref[...] = grad_middle
        grad_mix = grad_middle.astype(BF16)
        dmb_ref[...] = jnp.sum(grad_mix.astype(F32), 0, keepdims=True)
        gatt_ref[...] = dot_nt(grad_mix, wm_ref[...]).astype(BF16)
        size = att_refs[0].shape[1]
        for part, ref in enumerate(att_refs):
            sec_scr[part * size : (part + 1) * size, :] = ref[...].T
        put_rows(dw_refs, dot(sec_scr[...], grad_mix).astype(BF16), core)


def feed_backward(holders, core, grad_stream, hidden, second, vec, weights, apart, final=()):
    rows, width = grad_stream.shape
    array, at, mix_at = weights
    half = SLABS - EARLY if final else EARLY
    row = whole((1, width))
    small = jax.ShapeDtypeStruct((1, width), F32)
    base = EARLY if final else 0
    each = 2 if final else 1
    slab = lambda j: base + jnp.minimum(j // each, half - 1)
    blocks = 2 * half + 1 if final else 2 * half
    dw_specs, dw_shapes = grad_outs(holders, width, blocks * width, 2 * width // each, apart)
    square = whole((rows, width))
    in_specs = [
        pl.BlockSpec((rows, width), lambda j: (0, slab(j))),
        square,
        pl.BlockSpec((width, 2 * width), lambda j: (0, at // (2 * width) + slab(j))),
    ]
    operands = [hidden, second, array]
    out_specs = dw_specs + [pl.BlockSpec((1, width), lambda j: (0, slab(j) - base))]
    out_shape = dw_shapes + [jax.ShapeDtypeStruct((1, half * width), F32)]
    total = jax.ShapeDtypeStruct((rows, width), F32)
    scratch = [
        pltpu.VMEM((rows, width), BF16),
        pltpu.VMEM((width, rows), BF16),
        pltpu.VMEM((rows, width), BF16),
    ]
    attended = []
    if final:
        middle, attended, so_far = final
        in_specs += [
            square,
            vector(width, V_SG),
            pl.BlockSpec((width, width), lambda j: (0, mix_at // width)),
            square,
        ]
        operands += [middle, vec, array, so_far]
        out_specs += [square, square, row, row, row]
        out_shape += [total, jax.ShapeDtypeStruct((rows, width), BF16), small, small, small]
        scratch = [pltpu.VMEM((rows, width), F32)] + scratch
    else:
        out_specs += [square, row]
        out_shape += [total, small]
    return pl.pallas_call(
        functools.partial(feed_pull_kernel, bool(final), half, len(attended), len(dw_specs)),
        grid=(blocks if final else half,),
        in_specs=[pl.BlockSpec(memory_space=pltpu.SMEM), square]
        + [whole(piece.shape) for piece in attended]
        + in_specs,
        out_specs=out_specs,
        out_shape=out_shape,
        scratch_shapes=scratch,
        compiler_params=params(),
        cost_estimate=cost(blocks * 4 * rows * width * width, blocks * 5 * 2**20, rows * half * width),
        name="feed_backward",
    )(core, grad_stream, *attended, *operands)


def qkv_pull_kernel(parts, sums, outs, core_ref, *refs):
    dq_refs, refs = refs[:parts], refs[parts:]
    cont_refs, refs = refs[:parts], refs[parts:]
    sum_refs, refs = refs[: parts * sums], refs[parts * sums :]
    normed_ref, x_ref, gm_ref, gain_ref, w_ref = refs[:5]
    dw_refs = refs[5 : 5 + outs]
    out_ref, dbias_ref, dgain_ref, dshift_ref, norm_scr, acc_scr, g_scr = refs[5 + outs :]
    step = pl.program_id(0)

    @pl.when(step == 0)
    def _():
        norm_scr[...] = normed_ref[...].T
        acc_scr[...] = jnp.zeros_like(acc_scr)
        for part in range(parts):
            g_scr[part] = dq_refs[part][...]
            total = sum(ref[...].astype(F32) for ref in sum_refs[part * sums : (part + 1) * sums])
            for kind in range(2):
                both = jnp.concatenate([total[kind].astype(BF16), cont_refs[part][kind]], 0)
                g_scr[(1 + kind) * parts + part] = both

    grad = g_scr[step]
    dbias_ref[...] = jnp.sum(grad.astype(F32), 0, keepdims=True)
    put_rows(dw_refs, dot(norm_scr[...], grad).astype(BF16), core_ref[0])
    acc_scr[...] += dot_nt(grad, w_ref[...])

    @pl.when(step == pl.num_programs(0) - 1)
    def _():
        term, dgain, dshift = norm_pull(x_ref[...], gain_ref[...], acc_scr[...])
        dgain_ref[...] = dgain
        dshift_ref[...] = dshift
        out_ref[...] = gm_ref[...] + term


def qkv_backward(holders, core, dqs, conts, sums, normed, stream, grad_middle, vec, weights, apart):
    rows, width = stream.shape
    parts = len(dqs)
    block = width // parts
    wq, place = weights
    small = jax.ShapeDtypeStruct((1, width), F32)
    flat = [piece for part in sums for piece in part]
    dw_specs, dw_shapes = grad_outs(holders, width, 3 * width, block, apart)
    return pl.pallas_call(
        functools.partial(qkv_pull_kernel, parts, len(sums[0]), len(dw_specs)),
        grid=(3 * parts,),
        in_specs=[pl.BlockSpec(memory_space=pltpu.SMEM)]
        + [whole(piece.shape) for piece in dqs + conts + flat]
        + [
            whole((rows, width)),
            whole((rows, width)),
            whole((rows, width)),
            vector(width, V_FG),
            pl.BlockSpec((width, block), lambda j: (0, place // block + j)),
        ],
        out_specs=dw_specs
        + [
            whole((rows, width)),
            pl.BlockSpec((1, block), lambda j: (0, j)),
            whole((1, width)),
            whole((1, width)),
        ],
        out_shape=dw_shapes
        + [
            jax.ShapeDtypeStruct((rows, width), F32),
            jax.ShapeDtypeStruct((1, 3 * width), F32),
            small,
            small,
        ],
        scratch_shapes=[
            pltpu.VMEM((width, rows), BF16),
            pltpu.VMEM((rows, width), F32),
            pltpu.VMEM((3 * parts, rows, block), BF16),
        ],
        compiler_params=params(),
        cost_estimate=cost(12 * rows * width * width, 24 * 2**20),
        name="qkv_backward",
    )(core, *dqs, *conts, *flat, normed, stream, grad_middle, vec, wq)


def trade(block, axis, bits):
    return lax.ppermute(block, axis, [(i, i ^ bits) for i in range(lax.axis_size(axis))])


def from_others(block, n_tok):
    if n_tok != 4:
        return [trade(block, "tok", step) for step in range(1, n_tok)]
    first, second = trade(block, "tok", 1), trade(block, "tok", 2)
    half = block.shape[1] // 2
    third = [trade(first[:, :half], "tok", 2), trade(second[:, half:], "tok", 1)]
    return [first, second, jnp.concatenate(third, 1)]


def pick(block, place, axis):
    return lax.dynamic_index_in_dim(block, place, axis, keepdims=False)


def added(*blocks):
    return sum(block.astype(F32) for block in blocks).astype(BF16)


def split_kernel(count, lows, bits_ref, *refs):
    for side, low in enumerate(lows):
        ins = refs[side * count : (side + 1) * count]
        keep_ref, send_ref = refs[2 * count + 2 * side : 2 * count + 2 * side + 2]
        bit = bits_ref[side]
        for k in range(keep_ref.shape[1]):
            base = (k >> low << (low + 1)) | (k & ((1 << low) - 1))
            for ref, value in ((keep_ref, bit), (send_ref, 1 - bit)):
                place = base + (value << low)
                ref[:, k] = sum(one[:, place].astype(F32) for one in ins).astype(BF16)


def split_sum(sides, bits, lows, starts, cut):
    planes, holders, share, _ = sides[0][0].shape
    piece = next(size for size in range(cut, 0, -128) if all(start % size == 0 for start in starts))
    deep = max(1, planes // 2)
    specs = [
        pl.BlockSpec((deep, holders, share, piece), lambda i, j, start=start: (i, 0, 0, start // piece + j))
        for blocks, start in zip(sides, starts)
        for _ in blocks
    ]
    out = pl.BlockSpec((deep, holders // 2, share, piece), lambda i, j: (i, 0, 0, j))
    return pl.pallas_call(
        functools.partial(split_kernel, len(sides[0]), lows),
        grid=(planes // deep, cut // piece),
        in_specs=[pl.BlockSpec(memory_space=pltpu.SMEM)] + specs,
        out_specs=[out] * 4,
        out_shape=[jax.ShapeDtypeStruct((planes, holders // 2, share, cut), BF16)] * 4,
        compiler_params=params(("arbitrary",) * 2),
        cost_estimate=cost(planes * holders * share * cut * 4, 12 * planes * holders * share * cut),
        name="split_sum",
    )(jnp.stack(bits), *sides[0], *sides[1])


def plane_kernel(plane_ref, *refs):
    ins, outs = refs[:4], refs[4:]
    cut = ins[0].shape[-1]
    for step, ref in enumerate(outs):
        place = jnp.bitwise_xor(plane_ref[0], step)
        for side in range(2):
            value = ins[2 * side][place, 0].astype(F32) + ins[2 * side + 1][place, 0].astype(F32)
            ref[:, side * cut : (side + 1) * cut] = value.astype(BF16)


def plane_rows(blocks, plane):
    planes, _, share, cut = blocks[0].shape
    return pl.pallas_call(
        plane_kernel,
        grid=(1,),
        in_specs=[pl.BlockSpec(memory_space=pltpu.SMEM)] + [whole(block.shape) for block in blocks],
        out_specs=[whole((share, 2 * cut))] * planes,
        out_shape=[jax.ShapeDtypeStruct((share, 2 * cut), BF16)] * planes,
        compiler_params=params(),
        cost_estimate=cost(planes * share * cut * 4, planes * share * cut * 12),
        name="plane_rows",
    )(plane.reshape(1), *blocks)


def reduce_stages(*pairs):
    planes, span, columns = pairs[0][0].shape
    n_tok = lax.axis_size("tok")
    me, plane = lax.axis_index("tok"), lax.axis_index("wa") // 2
    bits = n_tok.bit_length() - 1
    cut = columns * len(pairs) // 2
    sides = [
        [
            block.reshape(planes, n_tok, span // n_tok, columns)
            for block in (mine, trade(other, "wa", 1))
        ]
        for mine, other in pairs
    ]
    starts = [0, 0]
    if len(pairs) == 1:
        sides, starts = sides * 2, [0, cut]
    orders = [list(range(bits)), list(reversed(range(bits)))]
    left = [list(range(bits)), list(range(bits))]
    for turn in range(bits):
        lows = []
        for order, rest in zip(orders, left):
            lows.append(rest.index(order[turn]))
            rest.remove(order[turn])
        own = [(me >> order[turn]) & 1 for order in orders]
        keep0, send0, keep1, send1 = split_sum(sides, own, lows, starts, cut)
        starts = [0, 0]
        sends = yield [send0, send1]
        sides = [
            [keep, trade(send, "tok", 1 << order[turn])]
            for keep, send, order in zip((keep0, keep1), sends, orders)
        ]
    sends = plane_rows(sides[0] + sides[1], plane)
    sends = yield sends
    got = [trade(send, "wa", 2 * step) for step, send in enumerate(sends) if step]
    return added(sends[0], *got)


def assemble_kernel(planes, holders, places_ref, *refs):
    own_ref, sibling_ref = refs[:2]
    near_refs, far_refs = refs[2 : 2 + holders], refs[2 + holders : 2 + 2 * holders]
    out_ref, sems = refs[-2:]
    wa, me = places_ref[0], places_ref[1]
    copies = []

    def copy(source, target):
        copies.append(pltpu.make_async_copy(source, target, sems.at[len(copies)]))
        copies[-1].start()

    copy(own_ref, out_ref.at[wa])
    copy(sibling_ref, out_ref.at[jnp.bitwise_xor(wa, 1)])
    for core, group in enumerate((near_refs, far_refs)):
        for turn, ref in enumerate(group):
            for step in range(1, planes):
                place = out_ref.at[jnp.bitwise_xor(wa, 2 * step + core), jnp.bitwise_xor(me, turn)]
                copy(ref.at[step - 1], place)
    for one in copies:
        one.wait()


def assemble(own, sibling, near, far):
    holders, share, columns = own.shape
    planes = near[0].shape[0] + 1
    anywhere = pl.BlockSpec(memory_space=pl.ANY)
    places = jnp.stack([lax.axis_index("wa"), lax.axis_index("tok")])
    whole_array = pl.pallas_call(
        functools.partial(assemble_kernel, planes, holders),
        in_specs=[pl.BlockSpec(memory_space=pltpu.SMEM)] + [anywhere] * (2 + 2 * holders),
        out_specs=anywhere,
        out_shape=jax.ShapeDtypeStruct((2 * planes, holders, share, columns), BF16),
        scratch_shapes=[pltpu.SemaphoreType.DMA((2 + 2 * holders * (planes - 1),))],
        compiler_params=pltpu.CompilerParams(vmem_limit_bytes=2**22),
        cost_estimate=cost(0, 8 * planes * holders * share * columns),
        name="assemble",
    )(places, own, sibling, *near, *far)
    return whole_array.reshape(-1, columns)


class Gathering:
    def __init__(self, shard):
        n_tok = lax.axis_size("tok")
        self.own = shard.reshape(n_tok, -1, shard.shape[1])
        self.ready = pick(self.own, lax.axis_index("tok"), 0)
        self.stage = 0

    def go(self, ready):
        planes, n_tok = lax.axis_size("wa") // 2, lax.axis_size("tok")
        if self.stage == 0:
            self.sibling = trade(self.own, "wa", 1)
            self.ready = jnp.stack([trade(ready, "wa", 2 * step) for step in range(1, planes)])
        elif self.stage == 1:
            self.near = [ready] + [trade(ready, "tok", step) for step in range(1, n_tok)]
            self.far = [trade(ready, "wa", 1)]
            self.ready = self.near
        elif self.stage == 2:
            self.near = ready
            self.far += [trade(block, "wa", 1) for block in ready[1:]]
            self.ready = None
        self.stage += 1

    def finish(self):
        while self.ready is not None:
            self.go(self.ready)
        return assemble(self.own, self.sibling, self.near, self.far)


def pack_kernel(span, me_ref, expand_ref, reduce_ref, mix_ref, qkv_ref, *out_refs):
    del me_ref
    width = mix_ref.shape[2]
    wide = (2 * SLABS + 1) * width
    for layer, out_ref in enumerate(out_refs):
        for a in range(SLABS):
            start = 2 * a * width
            for w in range(width // span):
                place = (w * SLABS + a) * span
                piece = expand_ref[layer, :, place : place + span]
                out_ref[:, start + w * span : start + (w + 1) * span] = piece
            out_ref[:, start + width : start + 2 * width] = reduce_ref[layer, a, 0]
        out_ref[:, wide - width : wide] = mix_ref[layer]
        if not layer:
            out_ref[:, wide:] = qkv_ref[1]


def pack(expand, reduce, mix, qkv):
    n_tok, me = lax.axis_size("tok"), lax.axis_index("tok")
    layers, span, width = mix.shape
    share = span // n_tok
    wide = (2 * SLABS + 1) * width
    by_row = lambda size: pl.BlockSpec((layers, share, size), lambda i, me: (0, me[0], 0))
    shapes = [(share, wide + 3 * width), (share, wide)]
    return pl.pallas_call(
        functools.partial(pack_kernel, span),
        grid_spec=pltpu.PrefetchScalarGridSpec(
            num_scalar_prefetch=1,
            grid=(1,),
            in_specs=[
                by_row(SLABS * width),
                pl.BlockSpec((layers, SLABS, 1, share, width), lambda i, me: (0, 0, me[0], 0, 0)),
                by_row(width),
                by_row(3 * width),
            ],
            out_specs=[pl.BlockSpec(shape, lambda i, me: (0, 0)) for shape in shapes],
        ),
        out_shape=[jax.ShapeDtypeStruct(shape, BF16) for shape in shapes],
        compiler_params=params(),
        cost_estimate=cost(0, 8 * share * wide),
        name="pack",
    )(
        me.reshape(1), expand, reduce.reshape(layers, SLABS, n_tok, share, width), mix, qkv
    )


class Reduction:
    def __init__(self, *pairs):
        self.walk = reduce_stages(*pairs)
        self.result = None
        self.ready = next(self.walk)

    def go(self, values):
        try:
            self.ready = self.walk.send(values)
        except StopIteration as stop:
            self.ready = None
            self.result = stop.value

    def finish(self):
        while self.ready is not None:
            self.go(self.ready)
        return self.result


def together(value, reductions):
    active = [item for item in reductions if item.ready is not None]
    value, ready = lax.optimization_barrier((value, [item.ready for item in active]))
    for item, values in zip(active, ready):
        item.go(values)
    return value


def feed_out_kernel(pieces, me_ref, *refs):
    mix_ref, expand_ref, reduce_ref = refs[-3:]
    span, width = mix_ref.shape[1] * mix_ref.shape[2], mix_ref.shape[3]
    for step in range(pieces):
        place = jnp.bitwise_xor(me_ref[0], step)
        early_ref, late_ref = refs[step], refs[pieces + step]
        for a in range(SLABS):
            ref, start = (early_ref, 2 * a) if a < EARLY else (late_ref, 2 * (a - EARLY))
            start *= width
            for w in range(width // span):
                value = ref[:, start + w * span : start + (w + 1) * span].astype(F32)
                expand_ref[0, place, :, (w * SLABS + a) * span : (w * SLABS + a + 1) * span] = value
            reduce_ref[0, a, place] = ref[:, start + width : start + 2 * width].astype(F32)
        mix_ref[0, place] = late_ref[:, 2 * (SLABS - EARLY) * width :].astype(F32)


def feed_out(early, late, width, me, layer, held):
    n_tok, share = len(early), early[0].shape[0]
    early_size, late_size = 2 * EARLY * width, (2 * (SLABS - EARLY) + 1) * width
    late_at = early_size // late_size if late[0].shape[1] > late_size else 0
    shapes = [(n_tok, share, width), (n_tok, share, SLABS * width), (SLABS, n_tok, share, width)]
    return pl.pallas_call(
        functools.partial(feed_out_kernel, n_tok),
        grid=(1,),
        in_specs=[pl.BlockSpec(memory_space=pltpu.SMEM)]
        + [whole((share, early_size)) for _ in early]
        + [pl.BlockSpec((share, late_size), lambda i: (0, late_at)) for _ in late]
        + [pl.BlockSpec(memory_space=pl.ANY) for _ in held],
        out_specs=[
            pl.BlockSpec((1,) + shape, lambda i, rank=len(shape): (layer,) + (0,) * rank)
            for shape in shapes
        ],
        out_shape=[jax.ShapeDtypeStruct((LAYERS,) + shape, F32) for shape in shapes],
        input_output_aliases={1 + 2 * n_tok + k: k for k in range(len(held))},
        compiler_params=params(),
        cost_estimate=cost(9 * share * n_tok * width, 6 * 9 * share * n_tok * width),
        name="feed_out",
    )(me.reshape(1), *early, *late, *held)


def qkv_out_kernel(pieces, me_ref, *refs):
    out_ref = refs[-1]
    for step, ref in enumerate(refs[:pieces]):
        out_ref[0, jnp.bitwise_xor(me_ref[0], step)] = ref[...].astype(F32)


def qkv_out(pieces, columns, me, layer, held):
    share = pieces[0].shape[0]
    shape = (len(pieces), share, columns)
    last = pieces[0].shape[1] // columns - 1
    return pl.pallas_call(
        functools.partial(qkv_out_kernel, len(pieces)),
        grid=(1,),
        in_specs=[pl.BlockSpec(memory_space=pltpu.SMEM)]
        + [pl.BlockSpec((share, columns), lambda i: (0, last)) for _ in pieces]
        + [pl.BlockSpec(memory_space=pl.ANY) for _ in held],
        out_specs=pl.BlockSpec((1,) + shape, lambda i: (layer, 0, 0, 0)),
        out_shape=jax.ShapeDtypeStruct((LAYERS,) + shape, F32),
        input_output_aliases={1 + len(pieces) + k: k for k in range(len(held))},
        compiler_params=params(),
        cost_estimate=cost(share * columns, 24 * share * columns),
        name="qkv_out",
    )(me.reshape(1), *pieces, *held)


def local(
    prompt_in, cont_in, first_gain, first_shift, qkv_weight, qv_bias, mix_weight, mix_bias,
    second_gain, second_shift, expand_weight, expand_bias, reduce_weight, reduce_bias, owners,
    prompt_cot, cont_cot,
):
    n_tok, n_wa = lax.axis_size("tok"), lax.axis_size("wa")
    me = lax.axis_index("tok")
    core = (lax.axis_index("wa") % 2).reshape(1)
    rows = prompt_in.shape[1]
    width = prompt_in.shape[2]
    span = width // n_wa
    parts = 2
    steps = list(range(1, n_tok))
    order = owners[0]
    by_step = jnp.stack([pick(order, me ^ step, 0) for step in [0] + steps])
    thr = (by_step[0] - by_step) * rows

    small = jnp.concatenate(
        [first_gain, first_shift, qv_bias, mix_bias, second_gain, second_shift, reduce_bias, expand_bias], 1
    )
    small = lax.all_gather(small, "wa", axis=0, tiled=False)

    def spread(layer):
        def piece(start, count):
            return small[:, layer, start * span : (start + count) * span].reshape(1, -1)

        pair = piece(2, 2)
        units = small[:, layer, 8 * span : 12 * span].reshape(n_wa, SLABS, span)
        pieces = [
            piece(0, 1), piece(1, 1), pair[:, :width], jnp.zeros((1, width), BF16), pair[:, width:],
            piece(4, 1), piece(5, 1), piece(6, 1), piece(7, 1),
            units.transpose(1, 0, 2).reshape(1, SLABS * width),
        ]
        return jnp.concatenate(pieces, 1).astype(F32)

    vecs = [spread(layer) for layer in range(LAYERS)]
    both = ("wa", "tok")
    share = span // n_tok

    wide = (2 * SLABS + 1) * width
    first = Gathering(qkv_weight[0])
    rows_middle, rows_last = pack(expand_weight, reduce_weight, mix_weight, qkv_weight)
    middle_array = lax.all_gather(rows_middle, both, axis=0, tiled=True)
    last_array = lax.all_gather(rows_last, both, axis=0, tiled=True)
    first = first.finish()

    stream = jnp.concatenate([prompt_in[0], cont_in[0, 0]], 0).astype(F32)
    kept = []
    size = width // parts
    weights = [
        ((first, 0), (middle_array, 0, wide - width)),
        ((middle_array, wide), (last_array, 0, wide - width)),
    ]
    for layer in range(LAYERS):
        wq, wf = weights[layer]
        qkv, normed = qkv_forward(stream, vecs[layer], *wq)
        fars, attended, lses = [], [], []
        for part in range(parts):
            block = jnp.stack(
                [
                    qkv[:rows, kind * width + part * size : kind * width + (part + 1) * size]
                    for kind in (1, 2)
                ]
            )
            fars.append(from_others(block, n_tok))
        for part in range(parts):
            one, lse = attend_forward(thr, qkv, fars[part], part, parts)
            attended.append(one)
            lses.append(lse)
        result, middle, second, hidden = feed_forward(stream, attended, vecs[layer], wf)
        kept.append((stream, normed, qkv, fars, lses, attended, middle, second, hidden))
        stream = result

    grad_stream = jnp.concatenate([prompt_cot[0], cont_cot[0, 0]], 0).astype(F32)
    smalls = [None] * LAYERS
    sync = lax.optimization_barrier

    def spread_rows(block):
        block = block.reshape(n_tok, share, block.shape[1])
        return [pick(block, me ^ step, 0) for step in [0] + steps]

    def from_each(blocks):
        return [blocks[0]] + [trade(block, "tok", step) for step, block in zip(steps, blocks[1:])]

    def to_each(block):
        return from_each([block] * n_tok)

    late, last, early = [None] * LAYERS, [None] * LAYERS, [None] * LAYERS
    for layer in reversed(range(LAYERS)):
        wq, wf = weights[layer]
        start, normed, qkv, fars, lses, attended, middle, second, hidden = kept[layer]
        if not layer:
            grad_stream = together(grad_stream, [late[1]])
        common = (n_wa, core, grad_stream, hidden, second, vecs[layer], wf)
        dw_early, deb_low, so_far, drb = feed_backward(*common, False)
        early[layer] = lax.psum_scatter(dw_early, "wa", scatter_dimension=0, tiled=True)
        if not layer:
            so_far, spread = together((so_far, spread_rows(early[1])), [late[1], last[1]])
            early[1] = added(*from_each(spread))
        late_mine, late_other, deb_high, grad_middle, grad_att, dsg, dss, dmb = feed_backward(
            *common, True, (middle, attended, so_far)
        )
        dqs, conts, sums = [], [], []
        for part in range(parts):
            if not layer:
                grad_att = together(grad_att, [last[1]])
            if layer or part:
                late[layer] = late[layer] or Reduction((late_mine, late_other))
            dq, cont, own, *far = attend_backward(
                thr, qkv, fars[part], lses[part], grad_att, attended[part], part, parts
            )
            dqs.append(dq)
            conts.append(cont)
            sums.append([own] + [trade(block, "tok", step) for step, block in zip(steps, far)])
        conts[-1] = together(conts[-1], [late[layer]])
        if not layer:
            upper = jnp.concatenate([early[1], late[1].finish(), last[1].finish()], 1)
            conts[-1], upper = sync((conts[-1], upper))
            upper = to_each(upper)
        *dwq, grad_stream, dqb, dfg, dfs = qkv_backward(
            n_wa, core, dqs, conts, sums, normed, start, grad_middle, vecs[layer], wq, bool(layer)
        )
        if layer:
            last[layer] = Reduction(dwq)
        else:
            last[layer] = lax.psum_scatter(dwq[0], "wa", scatter_dimension=0, tiled=True)
        dqb = jnp.concatenate([dqb[:, :width], dqb[:, 2 * width :]], 1)
        deb = jnp.concatenate([deb_low, deb_high], 1)
        deb = deb.reshape(SLABS, n_wa, span).transpose(1, 0, 2)
        smalls[layer] = [
            piece.reshape(n_wa, -1) for piece in (dfg, dfs, dqb, dmb, dsg, dss, deb, drb)
        ]

    small = jnp.stack([jnp.concatenate(pieces, 1) for pieces in smalls], 1)
    bits = n_wa.bit_length() - 1
    small = small.reshape((2,) * bits + small.shape[1:])
    for bit in reversed(range(bits)):
        place = (lax.axis_index("wa") >> bit) & 1
        small = pick(small, place, 0) + trade(pick(small, 1 - place, 0), "wa", 1 << bit)
    for step in [1 << bit for bit in range(n_tok.bit_length() - 1)]:
        small = small + trade(small, "tok", step)

    rows_early = together(spread_rows(early[0]), [late[0]])
    early[0] = to_each(added(*from_each(rows_early)))
    rows_late, last[0] = sync((late[0].finish(), spread_rows(last[0])))
    last[0] = added(*from_each(last[0]))
    feeds = feed_out(upper, upper, width, me, 1, [])
    qkvs = qkv_out(upper, 3 * width, me, 1, [])
    rows_late, early[0], feeds, qkvs = sync((to_each(rows_late), early[0], feeds, qkvs))
    feeds = feed_out(early[0], rows_late, width, me, 0, feeds)
    qkvs = qkv_out(to_each(last[0]), 3 * width, me, 0, [qkvs])
    mixes, expands, reduces = [
        block.reshape(LAYERS, -1, width) if place != 1 else block.reshape(LAYERS, span, -1)
        for place, block in enumerate(feeds)
    ]
    qkvs = qkvs.reshape(LAYERS, span, 3 * width)

    def vec_out(start, count):
        return small[:, start * span : (start + count) * span]

    return (
        stream[:rows][None],
        stream[rows:][None, None],
        grad_stream[:rows][None],
        grad_stream[rows:][None, None],
        vec_out(0, 1),
        vec_out(1, 1),
        qkvs,
        vec_out(2, 2),
        mixes,
        vec_out(4, 1),
        vec_out(5, 1),
        vec_out(6, 1),
        expands,
        vec_out(7, 4),
        reduces,
        vec_out(11, 1),
    )


def solution(mesh):
    in_specs = (
        P("wa", "tok", None),
        P("wa", "tok", None, None),
        P(None, "wa"),
        P(None, "wa"),
        P(None, "wa", None),
        P(None, "wa"),
        P(None, "wa", None),
        P(None, "wa"),
        P(None, "wa"),
        P(None, "wa"),
        P(None, "wa", None),
        P(None, "wa"),
        P(None, "wa", None),
        P(None, "wa"),
        P("wa", None),
        P("wa", "tok", None),
        P("wa", "tok", None, None),
    )
    out_specs = (
        P("wa", "tok", None),
        P("wa", "tok", None, None),
        P("wa", "tok", None),
        P("wa", "tok", None, None),
        P(None, "wa"),
        P(None, "wa"),
        P(None, "wa", None),
        P(None, "wa"),
        P(None, "wa", None),
        P(None, "wa"),
        P(None, "wa"),
        P(None, "wa"),
        P(None, "wa", None),
        P(None, "wa"),
        P(None, "wa", None),
        P(None, "wa"),
    )
    return jax.shard_map(local, mesh=mesh, in_specs=in_specs, out_specs=out_specs, check_vma=False)
```
